256 devices in a mesh: tm: 64 (over x, y_hi, z), band: 4 (over y_lo, core).
Axes of the slice: x: 4, y: 4 (y_hi: 2, y_lo: 2; y = y_hi * 2 + y_lo), z: 8, core: 2. Of those that a mesh axis runs over, the one named last changes fastest.
Arguments:
- spectrum: bfloat16 [1024, 8192], P('tm', 'band'), may hold values from -60 to 60
- band_assign: int32 [2, 1024, 60], replicated, may hold values from 0 to 1, as said below
- split_weight: bfloat16 [1024, 2, 8, 384], P('band'), may hold values from -0.375 to 0.375
- qkv_weight: bfloat16 [384, 1536], replicated, may hold values from -8 to 8
- out_weight: bfloat16 [512, 384], replicated, may hold values from -0.25 to 0.25
- mask_weight: bfloat16 [1024, 2, 8, 384], P('band'), may hold values from -0.3125 to 0.3125
- mask_cotangent: bfloat16 [1024, 8192], P('tm', 'band'), may hold values from -6 to 6
Outputs:
- band_mask: float32 [1024, 8192], P('tm', 'band')
- qkv_grad: float32 [384, 1536], replicated
- out_grad: float32 [512, 384], replicated
The draws below stay inside these ranges and needn't reach their ends.
Inputs may be any that keep to these rules, and one draw needn't show every extreme that they name: band_assign[0, f, b] = 1 where bin f lies on the rising side of band b and band_assign[1, f, b] = 1 where it lies on its falling side; each side is a run of consecutive bins, the falling side of band b is the rising side of band b + 1, and every bin lies on one or two sides.
All inputs are finite; a program needn't handle non-finite values.
Results may differ from the reference program's by a relative error of at most 0.02.
Values may be sent and summed in bfloat16 or wider, within the bound.
A program may use at most 128 MiB of HBM per device.

```python
import math
import jax
import jax.numpy as jnp
from jax import lax

D = 384
HEADS = 8
HEAD_DIM = 64
INNER = 512
BANDS = 60
BINS = 1024
BIN_FEATS = 8
FRAMES = 1024


def draw_spectrum(key, part):
    key = jax.random.fold_in(key, 11)
    key_values, key_frames, key_bins = jax.random.split(key, 3)
    raw_values = jnp.clip(jax.random.normal(key_values, (FRAMES, BINS, BIN_FEATS)), -6.0, 6.0)
    scale_low = 0.3
    scale_high = 3.0
    frame_scale = jnp.exp(jax.random.uniform(key_frames, (FRAMES, 1, 1), minval=math.log(scale_low), maxval=math.log(scale_high)))
    bin_scale = jnp.exp(jax.random.uniform(key_bins, (1, BINS, 1), minval=math.log(scale_low), maxval=math.log(scale_high)))
    return (raw_values * frame_scale * bin_scale).reshape(FRAMES, BINS * BIN_FEATS).astype(jnp.bfloat16)


def draw_qkv_weight(key, part):
    key = jax.random.fold_in(key, 5)
    key_matrix = jax.random.fold_in(key, 0)
    inner_width = HEADS * HEAD_DIM
    matrix = jnp.clip(jax.random.normal(key_matrix, (D, 3 * inner_width)), -6.0, 6.0) / math.sqrt(D)
    return matrix.astype(jnp.bfloat16)


def draw_band_assign(key, part):
    key = jax.random.fold_in(key, 7)
    segment_count = BANDS + 1
    segment_ids = jnp.arange(segment_count, dtype=jnp.int32)
    factors = jax.random.randint(key, (segment_count,), 4, 8).astype(jnp.int32)
    raw_sizes = (segment_ids + 8) * (segment_ids + 8) * factors
    spare_bins = BINS - 4 * segment_count
    seg_widths = 4 + spare_bins * raw_sizes // jnp.sum(raw_sizes)
    seg_widths = seg_widths.at[segment_count - 1].add(BINS - jnp.sum(seg_widths))
    seg_ends = jnp.cumsum(seg_widths).astype(jnp.int32)
    bin_ids = jnp.arange(BINS, dtype=jnp.int32)
    segment_of = jnp.sum((bin_ids[:, None] >= seg_ends[None, :]).astype(jnp.int32), axis=1)
    band_ids = jnp.arange(BANDS, dtype=jnp.int32)
    rising = (segment_of[:, None] == band_ids[None, :]).astype(jnp.int32)
    falling = (segment_of[:, None] == band_ids[None, :] + 1).astype(jnp.int32)
    return jnp.stack([rising, falling])


def steps_of(own_key, shape, cuts, least, top_value):
    factor_of = 1.0
    for dim, blocks in cuts:
        steps = jax.random.uniform(jax.random.fold_in(jax.random.fold_in(own_key, 6), dim), (blocks,), jnp.float32, least / len(cuts), top_value / len(cuts))
        factor_of = factor_of * jnp.repeat(jnp.exp(steps), shape[dim] // blocks).reshape((-1,) + (1,) * (len(shape) - 1 - dim))
    return factor_of


def gaussian(stream_key, dims, width, bound, cuts=(), kind=jnp.bfloat16):
    drawn = jax.random.normal(stream_key, dims, jnp.float32) * width
    if len(cuts) > 0:
        drawn = steps_of(stream_key, dims, cuts, -0.22, 0.18) * drawn
    return jnp.clip(drawn, min=-bound, max=bound).astype(kind)


def setup_inputs(seed: int = 0) -> dict:
    key_of = jax.random.split(jax.random.key(seed), 8)
    return {
        "spectrum": draw_spectrum(jax.random.fold_in(key_of[7], 71), 0),
        "band_assign": draw_band_assign(jax.random.fold_in(key_of[7], 71), 0),
        "split_weight": gaussian(key_of[2], (BINS, 2, BIN_FEATS, D), (2 * BINS * BIN_FEATS // BANDS) ** -0.5, 0.375, ((0, 4),)),
        "qkv_weight": draw_qkv_weight(jax.random.fold_in(key_of[7], 71), 0),
        "out_weight": gaussian(key_of[4], (INNER, D), INNER ** -0.5, 0.25),
        "mask_weight": gaussian(key_of[5], (BINS, 2, BIN_FEATS, D), D ** -0.5, 0.3125, ((0, 4),)),
        "mask_cotangent": gaussian(key_of[6], (FRAMES, BINS * BIN_FEATS), 1.0, 6.0, ((0, 64), (1, 4))),
    }


EPSILON = 1e-05

def rms_scaled(hidden):
    values = hidden.astype(jnp.float32)
    return values * lax.rsqrt(lax.optimization_barrier(jnp.mean(values * values, axis=-1, keepdims=True)) + EPSILON)

def rms_back(hidden, upstream):
    values = hidden.astype(jnp.float32)
    inverse = lax.rsqrt(lax.optimization_barrier(jnp.mean(values * values, axis=-1, keepdims=True)) + EPSILON)
    inner = lax.optimization_barrier(jnp.mean(upstream * values, axis=-1, keepdims=True))
    return inverse * upstream - values * (inverse * inverse * inverse) * inner

def rotary_tables(band_count, half_dim):
    position = jnp.arange(band_count).astype(jnp.float32)[:, None]
    frequency = jnp.exp(-math.log(10000.0) * jnp.arange(half_dim).astype(jnp.float32) / half_dim)[None, :]
    angles = position * frequency
    return (jnp.cos(angles)[None, :, None, :], jnp.sin(angles)[None, :, None, :])

def rotate(vectors, rot_cos, rot_sin):
    half_dim = vectors.shape[-1] // 2
    front_half = vectors[..., :half_dim]
    back_half = vectors[..., half_dim:]
    return jnp.concatenate([front_half * rot_cos - back_half * rot_sin, front_half * rot_sin + back_half * rot_cos], axis=-1)

def unrotate(vectors, rot_cos, rot_sin):
    half_dim = vectors.shape[-1] // 2
    front_half = vectors[..., :half_dim]
    back_half = vectors[..., half_dim:]
    return jnp.concatenate([front_half * rot_cos + back_half * rot_sin, back_half * rot_cos - front_half * rot_sin], axis=-1)

def layer_forward(hidden_in, qkv_weight, out_weight, head_count):
    frame_count, band_count, model_width = hidden_in.shape
    inner_width = qkv_weight.shape[1] // 3
    head_dim = inner_width // head_count
    normed_in = rms_scaled(hidden_in).astype(jnp.bfloat16).reshape(-1, model_width)
    projected = jnp.dot(normed_in, qkv_weight, preferred_element_type=jnp.float32)
    projected = projected.reshape(frame_count, band_count, 3, head_count, head_dim)
    rot_cos, rot_sin = rotary_tables(band_count, head_dim // 2)
    queries = rotate(projected[:, :, 0], rot_cos, rot_sin).astype(jnp.bfloat16)
    key_vecs = rotate(projected[:, :, 1], rot_cos, rot_sin).astype(jnp.bfloat16)
    values = projected[:, :, 2].astype(jnp.bfloat16)
    scores = jnp.einsum('tihe,tjhe->thij', queries.astype(jnp.float32), key_vecs.astype(jnp.float32)) * head_dim ** (-0.5)
    attn_probs = jax.nn.softmax(scores, axis=-1)
    probs_bf = attn_probs.astype(jnp.bfloat16)
    attended = jnp.einsum('thij,tjhe->tihe', probs_bf.astype(jnp.float32), values.astype(jnp.float32))
    attended = attended.astype(jnp.bfloat16).reshape(-1, inner_width)
    mixed = jnp.dot(attended, out_weight, preferred_element_type=jnp.float32)
    hidden_out = (hidden_in.astype(jnp.float32) + mixed.reshape(hidden_in.shape)).astype(jnp.bfloat16)
    return (hidden_out, (normed_in, queries, key_vecs, values, attn_probs, probs_bf, attended))

def layer_back(grad_flat, stored, out_weight):
    normed_in, queries, key_vecs, values, attn_probs, probs_bf, attended = stored
    band_count = queries.shape[1]
    head_dim = queries.shape[3]
    out_grad = jnp.dot(attended.T, grad_flat, preferred_element_type=jnp.float32)
    grad_attended = jnp.dot(grad_flat, out_weight.T, preferred_element_type=jnp.float32)
    grad_attended = grad_attended.astype(jnp.bfloat16).reshape(queries.shape).astype(jnp.float32)
    grad_probs = jnp.einsum('tihe,tjhe->thij', grad_attended, values.astype(jnp.float32))
    grad_values = jnp.einsum('thij,tihe->tjhe', probs_bf.astype(jnp.float32), grad_attended)
    grad_scores = attn_probs * (grad_probs - lax.optimization_barrier(jnp.sum(grad_probs * attn_probs, axis=-1, keepdims=True))) * head_dim ** (-0.5)
    grad_scores = grad_scores.astype(jnp.bfloat16).astype(jnp.float32)
    grad_queries = jnp.einsum('thij,tjhe->tihe', grad_scores, key_vecs.astype(jnp.float32))
    grad_keys = jnp.einsum('thij,tihe->tjhe', grad_scores, queries.astype(jnp.float32))
    rot_cos, rot_sin = rotary_tables(band_count, head_dim // 2)
    grad_projected = jnp.stack([unrotate(grad_queries, rot_cos, rot_sin), unrotate(grad_keys, rot_cos, rot_sin), grad_values], axis=2)
    grad_projected = grad_projected.astype(jnp.bfloat16).reshape(normed_in.shape[0], -1)
    qkv_grad = jnp.dot(normed_in.T, grad_projected, preferred_element_type=jnp.float32)
    return (qkv_grad, out_grad)

def reference(spectrum, band_assign, split_weight, qkv_weight, out_weight, mask_weight, mask_cotangent):
    frame_total = spectrum.shape[0]
    bin_count = split_weight.shape[0]
    bin_feats = split_weight.shape[2]
    model_width = split_weight.shape[3]
    inner_width = out_weight.shape[0]
    band_count = band_assign.shape[2]
    band_index = lax.optimization_barrier(jnp.sum(band_assign * jnp.arange(band_count).astype(jnp.int32)[None, None, :], axis=2)).astype(jnp.int32).reshape(-1)
    member = lax.optimization_barrier(jnp.sum(band_assign, axis=2)).astype(jnp.float32)
    member_flat = member.reshape(-1)
    cover = lax.optimization_barrier(jnp.sum(member, axis=0))
    band_sizes = bin_feats * lax.optimization_barrier(jnp.sum(band_assign, axis=(0, 1))).astype(jnp.float32)
    block_size = math.gcd(frame_total, 16)
    block_count = frame_total // block_size

    def one_block(totals, inputs):
        spec_rows, grad_rows = inputs
        spec = spec_rows.reshape(block_size, bin_count, bin_feats).astype(jnp.float32)
        contrib = jnp.einsum('tfc,fscd->sftd', spec, split_weight.astype(jnp.float32)).astype(jnp.bfloat16)
        gathered = contrib.astype(jnp.float32).reshape(2 * bin_count, block_size, model_width) * member_flat[:, None, None]
        summed = jnp.transpose(jax.ops.segment_sum(gathered, band_index, num_segments=band_count), (1, 0, 2))
        squares = lax.optimization_barrier(jnp.sum(spec * spec, axis=2))
        square_terms = (member[:, :, None] * squares.T[None, :, :]).reshape(2 * bin_count, block_size)
        energy = jax.ops.segment_sum(square_terms, band_index, num_segments=band_count).T
        hidden_in = (summed * lax.rsqrt(energy / band_sizes[None, :] + EPSILON)[:, :, None]).astype(jnp.bfloat16)
        hidden_out, stored = layer_forward(hidden_in, qkv_weight, out_weight, HEADS)
        normed_out = rms_scaled(hidden_out).astype(jnp.bfloat16)
        picked = jnp.take(normed_out, band_index, axis=1).reshape(block_size, 2, bin_count, model_width)
        picked = picked * member.astype(jnp.bfloat16)[None, :, :, None]
        estimate = jnp.einsum('tsfd,fscd->tfc', picked.astype(jnp.float32), mask_weight.astype(jnp.float32))
        estimate = (estimate / cover[None, :, None]).reshape(block_size, bin_count * bin_feats)
        scaled = (grad_rows.reshape(block_size, bin_count, bin_feats).astype(jnp.float32) / cover[None, :, None]).astype(jnp.bfloat16)
        grad_picked = jnp.einsum('tfc,fscd->sftd', scaled.astype(jnp.float32), mask_weight.astype(jnp.float32)).astype(jnp.bfloat16)
        grad_terms = grad_picked.astype(jnp.float32).reshape(2 * bin_count, block_size, model_width) * member_flat[:, None, None]
        grad_normed = jnp.transpose(jax.ops.segment_sum(grad_terms, band_index, num_segments=band_count), (1, 0, 2))
        grad_flat = rms_back(hidden_out, grad_normed).astype(jnp.bfloat16).reshape(-1, model_width)
        qkv_grad, out_grad = layer_back(grad_flat, stored, out_weight)
        return ((totals[0] + qkv_grad, totals[1] + out_grad), estimate)
    start = (jnp.zeros((model_width, 3 * inner_width), jnp.float32), jnp.zeros((inner_width, model_width), jnp.float32))
    inputs = (spectrum.reshape(block_count, block_size, -1), mask_cotangent.reshape(block_count, block_size, -1))
    totals, estimates = lax.scan(one_block, start, inputs)
    return (estimates.reshape(frame_total, -1), totals[0], totals[1])
```

```python
import functools
import math

import jax
import jax.numpy as jnp
import numpy as np
from jax import lax
from jax.experimental import pallas as pl
from jax.experimental.pallas import tpu as pltpu
from jax.sharding import PartitionSpec as P

HEADS = 8
HEAD_DIM = 64
HALF = 32
D = 384
INNER = 512
BANDS = 60
PAD = 64
FEATS = 8
EPSILON = 1e-05
VMEM_BYTES = 50 * 1024 * 1024
BF16 = jnp.bfloat16
F32 = jnp.float32

NN = (((1,), (0,)), ((), ()))
NT = (((1,), (1,)), ((), ()))
TN = (((0,), (0,)), ((), ()))


def dot(left, right, dims=NN):
    return lax.dot_general(left, right, dims, preferred_element_type=F32)


def split_three(values):
    high = values.astype(BF16)
    rest = values - high.astype(F32)
    middle = rest.astype(BF16)
    low = (rest - middle.astype(F32)).astype(BF16)
    return high, middle, low


def iota(shape, dim):
    return lax.broadcasted_iota(jnp.int32, shape, dim)


def segment_masks(assign_ref, bin_count):
    first_bin = pl.multiple_of(lax.axis_index("band") * bin_count, bin_count)
    rising = assign_ref[0, pl.ds(first_bin, bin_count), :].astype(BF16)
    falling = assign_ref[1, pl.ds(first_bin, bin_count), :].astype(BF16)
    row, column = iota((PAD, BANDS), 0), iota((PAD, BANDS), 1)
    same = jnp.where(row == column, 1.0, 0.0).astype(BF16)
    last = jnp.where((row == BANDS) & (column == BANDS - 1), 1.0, 0.0).astype(BF16)
    segments = dot(same, rising, NT) + dot(last, falling, NT)
    bands = dot(same, rising, NT) + dot(same, falling, NT)
    width = bin_count * FEATS
    repeat = jnp.where(
        iota((bin_count, width), 1) // FEATS == iota((bin_count, width), 0), 1.0, 0.0
    ).astype(BF16)
    segment_mask = dot(segments.astype(BF16), repeat)
    band_mask = dot(bands.astype(BF16), repeat)
    cover = jnp.sum(band_mask, axis=0, keepdims=True)
    return segment_mask, band_mask, cover


def pack_weight(weight_ref, packed_ref):
    bin_count = weight_ref.shape[0]
    step = 32
    for first in range(0, bin_count, step):
        for side in range(2):
            block = weight_ref[first : first + step, side].astype(F32)
            packed_ref[first * FEATS : (first + step) * FEATS, side * D : (side + 1) * D] = (
                block.reshape(step * FEATS, D).astype(BF16)
            )


def masked_sums(rows_ref, mask, packed_ref, out_ref, masked_ref):
    quarter_rows = out_ref.shape[1]
    frames = quarter_rows // PAD
    in_band = iota((quarter_rows, 1), 0) % PAD < BANDS
    for quarter in range(out_ref.shape[0]):
        for frame in range(frames):
            row = rows_ref[quarter * frames + frame : quarter * frames + frame + 1, :]
            masked_ref[frame * PAD : (frame + 1) * PAD, :] = mask * row
        total = dot(masked_ref[...], packed_ref[...])
        shifted = pltpu.roll(total[:, D:], quarter_rows - 1, 0)
        out_ref[quarter] = jnp.where(in_band, total[:, :D] + shifted, 0.0).astype(BF16)


def split_kernel(
    spectrum_ref,
    cotangent_ref,
    assign_ref,
    split_ref,
    mask_ref,
    summed_ref,
    grad_ref,
    energy_ref,
    segment_ref,
    cover_ref,
    mask_packed_ref,
    split_packed_ref,
    masked_ref,
):
    bin_count = split_ref.shape[0]
    segment_mask, band_mask, cover = segment_masks(assign_ref, bin_count)
    segment_bf = segment_mask.astype(BF16)
    segment_ref[...] = segment_bf
    inverse = 1.0 / cover
    cover_ref[...] = inverse
    spectrum = spectrum_ref[...].astype(F32)
    band_bf = band_mask.astype(BF16)
    energy = jnp.zeros((spectrum.shape[0], PAD), F32)
    for term in split_three(spectrum * spectrum):
        energy += dot(term, band_bf, NT)
    energy_ref[...] = jnp.zeros_like(energy_ref)
    energy_ref[:, :PAD] = energy
    pack_weight(split_ref, split_packed_ref)
    masked_sums(spectrum_ref, segment_bf, split_packed_ref, summed_ref, masked_ref)
    pack_weight(mask_ref, mask_packed_ref)
    scaled = (segment_mask * inverse).astype(BF16)
    masked_sums(cotangent_ref, scaled, mask_packed_ref, grad_ref, masked_ref)


def remote(source, target, send, receive, index, device):
    return pltpu.make_async_remote_copy(
        src_ref=source,
        dst_ref=target,
        send_sem=send.at[index],
        recv_sem=receive.at[index],
        device_id=device,
        device_id_type=pl.DeviceIdType.MESH,
    )


def enter(devices):
    barrier = pltpu.get_barrier_semaphore()
    for device in devices:
        pl.semaphore_signal(
            barrier, inc=1, device_id=device, device_id_type=pl.DeviceIdType.MESH
        )
    pl.semaphore_wait(barrier, len(devices))


def reduce_kernel(
    summed_ref,
    grad_ref,
    energy_ref,
    summed_out,
    grad_out,
    energy_out,
    from_core,
    to_chip,
    from_chip,
    energies,
    send,
    receive,
):
    me_tm, me = lax.axis_index("tm"), lax.axis_index("band")
    chip, core = me // 2, me % 2
    other_core = (me_tm, chip * 2 + 1 - core)
    other_chip = (me_tm, (1 - chip) * 2 + core)
    peers = [(me_tm, lax.rem(me + step, 4)) for step in (1, 2, 3)]
    enter(peers)
    inputs, outputs = (summed_ref, grad_ref), (summed_out, grad_out)
    copies = []
    for slot, peer in enumerate(peers):
        copy = remote(energy_ref, energies.at[slot], send, receive, slot, peer)
        copy.start()
        copies.append(copy)
    first, second, across = [], [], []
    for item in range(2):
        copy = remote(
            inputs[item].at[(1 - chip) * 2 + 1 - core],
            from_core.at[item, 0],
            send,
            receive,
            3 + item,
            other_core,
        )
        copy.start()
        first.append(copy)
    for item in range(2):
        copy = remote(
            inputs[item].at[chip * 2 + 1 - core],
            from_core.at[item, 1],
            send,
            receive,
            5 + item,
            other_core,
        )
        copy.start()
        second.append(copy)
    for item in range(2):
        first[item].wait_recv()
        to_chip[item] = (
            inputs[item][(1 - chip) * 2 + core].astype(F32) + from_core[item, 0].astype(F32)
        ).astype(BF16)
        copy = remote(to_chip.at[item], from_chip.at[item], send, receive, 7 + item, other_chip)
        copy.start()
        across.append(copy)
    for copy in copies:
        copy.wait_recv()
    energy_out[...] = energy_ref[...] + energies[0] + energies[1] + energies[2]
    for item in range(2):
        second[item].wait_recv()
        across[item].wait_recv()
        outputs[item][...] = (
            inputs[item][chip * 2 + core].astype(F32) + from_core[item, 1].astype(F32)
        ) + from_chip[item].astype(F32)
    for copy in copies + first + second + across:
        copy.wait_send()


def layer_kernel(
    summed_ref,
    grad_ref,
    energy_ref,
    assign_ref,
    qkv_ref,
    out_weight_ref,
    table_ref,
    normed_ref,
    weight_grad_ref,
    probs_ref,
    heads_ref,
    attended_ref,
    grad_projected_ref,
):
    tokens = summed_ref.shape[0]
    frames = tokens // PAD
    me = lax.axis_index("band")
    sizes = FEATS * jnp.sum(
        (assign_ref[0] + assign_ref[1]).astype(F32), axis=0, keepdims=True
    )
    ratio = energy_ref[:, :BANDS] / jnp.maximum(sizes, 1.0)
    lane = iota((BANDS, tokens), 1)
    spread = jnp.where(lane % PAD == iota((BANDS, tokens), 0), 1.0, 0.0).astype(BF16)
    rows = energy_ref.shape[0]
    energy = jnp.zeros((rows, tokens), F32)
    for term in split_three(ratio):
        energy += dot(term, spread)
    mine = iota((rows, tokens), 0) == me * frames + iota((rows, tokens), 1) // PAD
    energy = jnp.sum(jnp.where(mine, energy, 0.0), axis=0, keepdims=True)
    in_band = iota((1, tokens), 1) % PAD < BANDS

    hidden_in = (jnp.transpose(summed_ref[...]) * lax.rsqrt(energy + EPSILON)).astype(BF16)
    hidden_in = hidden_in.astype(F32)
    normed_in = (
        hidden_in
        * lax.rsqrt(jnp.mean(hidden_in * hidden_in, axis=0, keepdims=True) + EPSILON)
    ).astype(BF16)
    projected = dot(qkv_ref[...], normed_in, TN)
    cos, sin = table_ref[:HALF, :], table_ref[HALF:, :]
    scale = HEAD_DIM**-0.5
    key_lane, query_lane = iota((tokens, tokens), 0), iota((tokens, tokens), 1)
    allowed = (key_lane // PAD == query_lane // PAD) & (key_lane % PAD < BANDS)
    bias = jnp.where(allowed, 0.0, -1e30)
    for head in range(HEADS):
        for part in range(2):
            base = part * INNER + head * HEAD_DIM
            front = projected[base : base + HALF]
            back = projected[base + HALF : base + HEAD_DIM]
            factor = scale if part == 0 else 1.0
            heads_ref[base : base + HALF, :] = ((front * cos - back * sin) * factor).astype(BF16)
            heads_ref[base + HALF : base + HEAD_DIM, :] = (
                (front * sin + back * cos) * factor
            ).astype(BF16)
    heads_ref[2 * INNER :, :] = projected[2 * INNER :].astype(BF16)

    def part_of(part, head):
        base = part * INNER + head * HEAD_DIM
        return heads_ref[base : base + HEAD_DIM, :]

    for head in range(HEADS):
        scores = dot(part_of(1, head), part_of(0, head), TN) + bias
        powers = jnp.exp(scores - jnp.max(scores, axis=0, keepdims=True))
        probs = powers / jnp.sum(powers, axis=0, keepdims=True)
        probs_ref[head] = probs
        attended_ref[head * HEAD_DIM : (head + 1) * HEAD_DIM, :] = dot(
            part_of(2, head), probs.astype(BF16)
        ).astype(BF16)
    mixed = dot(out_weight_ref[...], attended_ref[...], TN)
    hidden_out = (hidden_in + mixed).astype(BF16).astype(F32)
    inverse = lax.rsqrt(jnp.mean(hidden_out * hidden_out, axis=0, keepdims=True) + EPSILON)
    normed_out = jnp.where(in_band, hidden_out * inverse, 0.0)
    normed_ref[...] = jnp.transpose(normed_out).astype(BF16)

    upstream = jnp.transpose(grad_ref[...])
    inner = jnp.mean(upstream * hidden_out, axis=0, keepdims=True)
    grad_hidden = (
        inverse * upstream - hidden_out * (inverse * inverse * inverse) * inner
    ).astype(BF16)
    grad_attended = dot(out_weight_ref[...], grad_hidden).astype(BF16)
    out_grad = dot(attended_ref[...], grad_hidden, NT).astype(BF16)
    quarter = INNER // 4
    for block in range(4):
        weight_grad_ref[D:, block * D : (block + 1) * D] = out_grad[
            block * quarter : (block + 1) * quarter
        ]
    for head in range(HEADS):
        probs = probs_ref[head]
        grad_head = grad_attended[head * HEAD_DIM : (head + 1) * HEAD_DIM]
        grad_probs = dot(part_of(2, head), grad_head, TN)
        row_sum = jnp.sum(grad_probs * probs, axis=0, keepdims=True)
        grad_scores = (probs * (grad_probs - row_sum)).astype(BF16)
        grad_values = dot(grad_head, probs.astype(BF16), NT)
        grad_queries = dot(part_of(1, head), grad_scores) * scale
        grad_keys = dot(part_of(0, head), grad_scores, NT)
        for part, grad in ((0, grad_queries), (1, grad_keys)):
            base = part * INNER + head * HEAD_DIM
            front, back = grad[:HALF], grad[HALF:]
            grad_projected_ref[base : base + HALF, :] = (front * cos + back * sin).astype(BF16)
            grad_projected_ref[base + HALF : base + HEAD_DIM, :] = (
                back * cos - front * sin
            ).astype(BF16)
        base = 2 * INNER + head * HEAD_DIM
        grad_projected_ref[base : base + HEAD_DIM, :] = grad_values.astype(BF16)
    weight_grad_ref[:D, :] = dot(normed_in, grad_projected_ref[...], NT).astype(BF16)


def total_kernel(
    sizes,
    normed_ref,
    grad_ref,
    normed_out,
    grad_out,
    normed_all,
    gathered,
    core_in,
    pair_sum,
    first_in,
    first_sum,
    second_in,
    second_sum,
    depth_in,
    depth_all,
    second_all,
    send,
    receive,
):
    x_size, y_high, z_size = sizes
    y_size = y_high * 2
    me_tm, me = lax.axis_index("tm"), lax.axis_index("band")
    chip, core = me // 2, me % 2
    x = me_tm // (y_high * z_size)
    y = (me_tm // z_size) % y_high * 2 + chip
    z = me_tm % z_size

    def device(at_x, at_y, at_z, at_core):
        return ((at_x * y_high + at_y // 2) * z_size + at_z, (at_y % 2) * 2 + at_core)

    other_core = device(x, y, z, 1 - core)
    x_peers = [device(lax.rem(x + s, x_size), y, z, core) for s in range(1, x_size)]
    y_peers = [device(x, lax.rem(y + s, y_size), z, core) for s in range(1, y_size)]
    z_peers = [device(x, y, lax.rem(z + s, z_size), core) for s in range(1, z_size)]
    other_chip = (me_tm, (1 - chip) * 2 + core)
    enter([other_core] + x_peers + y_peers + z_peers)
    next_index = [0]
    started = []

    def begin(source, target, to):
        copy = remote(source, target, send, receive, next_index[0], to)
        next_index[0] += 1
        copy.start()
        started.append(copy)
        return copy

    half = grad_ref.shape[0] // 2
    columns = grad_ref.shape[1] // 2
    left, right = pl.ds(0, columns), pl.ds(columns, columns)

    normed_all[me] = normed_ref[...]
    pair_copy = begin(
        grad_ref.at[pl.ds(pl.multiple_of((1 - core) * half, half), half), :], core_in, other_core
    )
    to_chip = begin(normed_ref, normed_all.at[me], other_chip)
    to_core = begin(normed_ref, normed_all.at[me], other_core)

    pair_copy.wait_recv()
    own = pl.ds(pl.multiple_of(core * half, half), half)
    pair_sum[...] = (grad_ref[own, :].astype(F32) + core_in[...].astype(F32)).astype(BF16)

    axes = ((x, x_size, x_peers), (y, y_size, y_peers))
    rows = [half // x_size, half // y_size]
    firsts = ([], [])
    for step in range(max(x_size, y_size) - 1):
        for part in range(2):
            at, size, peers = axes[part]
            if step < size - 1:
                count = rows[part]
                there = pl.ds(pl.multiple_of(lax.rem(at + step + 1, size) * count, count), count)
                firsts[part].append(
                    begin(
                        pair_sum.at[there, (left, right)[part]],
                        first_in[part].at[step],
                        peers[step],
                    )
                )
    for part in range(2):
        at, size, peers = axes[part]
        count = rows[part]
        here = pl.ds(pl.multiple_of(at * count, count), count)
        total = pair_sum[here, (left, right)[part]].astype(F32)
        for step in range(size - 1):
            firsts[part][step].wait_recv()
            total += first_in[part][step].astype(F32)
        first_sum[part][...] = total.astype(BF16)

    last_rows = half // (x_size * y_size)
    seconds = ([], [])
    for part in range(2):
        at, size, peers = axes[1 - part]
        for step in range(size - 1):
            there = pl.ds(
                pl.multiple_of(lax.rem(at + step + 1, size) * last_rows, last_rows), last_rows
            )
            seconds[part].append(
                begin(first_sum[part].at[there, :], second_in[part].at[step], peers[step])
            )
    chunk_rows, chunk_columns = 8, columns // 2
    for part in range(2):
        at, size, peers = axes[1 - part]
        here = pl.ds(pl.multiple_of(at * last_rows, last_rows), last_rows)
        total = first_sum[part][here, :].astype(F32)
        for step in range(size - 1):
            seconds[part][step].wait_recv()
            total += second_in[part][step].astype(F32)
        if z_size == 1:
            second_all[part][here, :] = total.astype(BF16)
        else:
            for block in range(4):
                r, c = block // 2 * chunk_rows, block % 2 * chunk_columns
                second_sum[part * 4 + block] = total[r : r + chunk_rows, c : c + chunk_columns]

    if z_size > 1:
        depths = [
            begin(second_sum.at[lax.rem(z + s, z_size)], depth_in.at[s - 1], z_peers[s - 1])
            for s in range(1, z_size)
        ]
        total = second_sum[z]
        for step in range(z_size - 1):
            depths[step].wait_recv()
            total += depth_in[step]
        depth_all[z] = total
        backs = [begin(depth_all.at[z], depth_all.at[z], peer) for peer in z_peers]
        for copy in backs:
            copy.wait_recv()
        for part in range(2):
            at = axes[1 - part][0]
            here = pl.ds(pl.multiple_of(at * last_rows, last_rows), last_rows)
            rows_of = []
            for high in range(2):
                rows_of.append(
                    jnp.concatenate(
                        [depth_all[part * 4 + high * 2], depth_all[part * 4 + high * 2 + 1]], axis=1
                    )
                )
            second_all[part][here, :] = jnp.concatenate(rows_of, axis=0).astype(BF16)

    backs = ([], [])
    for part in range(2):
        at, size, peers = axes[1 - part]
        here = pl.ds(pl.multiple_of(at * last_rows, last_rows), last_rows)
        for peer in peers:
            backs[part].append(
                begin(second_all[part].at[here, :], second_all[part].at[here, :], peer)
            )
    to_chip.wait_recv()
    onward = begin(
        normed_all.at[(1 - chip) * 2 + core], normed_all.at[(1 - chip) * 2 + core], other_core
    )
    spread = ([], [])
    mirrored = []
    base = core * half
    for part in range(2):
        for copy in backs[part]:
            copy.wait_recv()
        at, size, peers = axes[part]
        count = rows[part]
        here = pl.ds(pl.multiple_of(base + at * count, count), count)
        target = gathered.at[here, (left, right)[part]]
        for peer in peers:
            spread[part].append(begin(second_all[part], target, peer))
        gathered[here, (left, right)[part]] = second_all[part][...]
        mirrored.append(begin(second_all[part], target, other_core))
    for step in range(max(x_size, y_size) - 1):
        for part in range(2):
            at, size, peers = axes[part]
            if step < size - 1:
                count = rows[part]
                spread[part][step].wait_recv()
                origin = lax.rem(at + size - step - 1, size)
                here = pl.ds(pl.multiple_of(base + origin * count, count), count)
                block = gathered.at[here, (left, right)[part]]
                mirrored.append(begin(block, block, other_core))
    to_core.wait_recv()
    onward.wait_recv()
    normed_out[...] = normed_all[...]
    for copy in mirrored:
        copy.wait_recv()
    grad_out[...] = gathered[...]
    for copy in started:
        copy.wait_send()


def mask_kernel(normed_ref, segment_ref, cover_ref, packed_ref, out_ref, pair_ref):
    quarter_rows = normed_ref.shape[1]
    frames = quarter_rows // PAD
    mask = segment_ref[...].astype(F32)
    inverse = cover_ref[...]
    for quarter in range(normed_ref.shape[0]):
        normed = normed_ref[quarter]
        pair_ref[:, :D] = normed
        pair_ref[:, D:] = pltpu.roll(normed.astype(F32), 1, 0).astype(BF16)
        estimate = dot(pair_ref[...], packed_ref[...], NT)
        for frame in range(frames):
            rows = estimate[frame * PAD : (frame + 1) * PAD]
            out_ref[quarter * frames + frame : quarter * frames + frame + 1, :] = (
                jnp.sum(rows * mask, axis=0, keepdims=True) * inverse
            )


VMEM = pl.BlockSpec(memory_space=pltpu.VMEM)


def call(kernel, outs, ins, scratch, **params):
    return pl.pallas_call(
        kernel,
        out_shape=outs,
        in_specs=[VMEM] * ins,
        out_specs=[VMEM] * len(outs),
        scratch_shapes=scratch,
        compiler_params=pltpu.CompilerParams(vmem_limit_bytes=VMEM_BYTES, **params),
    )


def rotary_table(tokens):
    position = (np.arange(tokens) % PAD).astype(np.float64)[None, :]
    frequency = np.exp(-math.log(10000.0) * np.arange(HALF) / HALF)[:, None]
    angles = position * frequency
    return np.concatenate([np.cos(angles), np.sin(angles)], axis=0).astype(np.float32)


def axis_sizes(tm_size):
    return {64: (4, 2, 8), 8: (4, 2, 1), 4: (4, 1, 1), 2: (2, 1, 1), 1: (1, 1, 1)}[tm_size]


def on_device(
    sizes, spectrum, band_assign, split_weight, qkv_weight, out_weight, mask_weight, mask_cotangent
):
    frames, width = spectrum.shape
    quarter = frames // 4 * PAD
    shape = jax.ShapeDtypeStruct
    summed, grad, energy, segment, cover, packed = call(
        split_kernel,
        [
            shape((4, quarter, D), BF16),
            shape((4, quarter, D), BF16),
            shape((frames, 128), F32),
            shape((PAD, width), BF16),
            shape((1, width), F32),
            shape((width, 2 * D), BF16),
        ],
        5,
        [pltpu.VMEM((width, 2 * D), BF16), pltpu.VMEM((quarter, width), BF16)],
    )(spectrum, mask_cotangent, band_assign, split_weight, mask_weight)
    summed, grad, energy = call(
        reduce_kernel,
        [shape((quarter, D), F32), shape((quarter, D), F32), shape((frames, 128), F32)],
        3,
        [
            pltpu.VMEM((2, 2, quarter, D), BF16),
            pltpu.VMEM((2, quarter, D), BF16),
            pltpu.VMEM((2, quarter, D), BF16),
            pltpu.VMEM((3, frames, 128), F32),
            pltpu.SemaphoreType.DMA((9,)),
            pltpu.SemaphoreType.DMA((9,)),
        ],
        collective_id=0,
        has_side_effects=True,
    )(summed, grad, energy)
    normed, weight_grad = call(
        layer_kernel,
        [shape((quarter, D), BF16), shape((INNER, 4 * D), BF16)],
        7,
        [
            pltpu.VMEM((HEADS, quarter, quarter), F32),
            pltpu.VMEM((3 * INNER, quarter), BF16),
            pltpu.VMEM((INNER, quarter), BF16),
            pltpu.VMEM((3 * INNER, quarter), BF16),
        ],
    )(
        summed,
        grad,
        energy,
        band_assign,
        qkv_weight,
        out_weight,
        jnp.asarray(rotary_table(quarter)),
    )
    x_size, y_high, z_size = sizes
    y_size = 2 * y_high
    half, columns = INNER // 2, 2 * D
    last = half // (x_size * y_size)
    copies = 64
    normed_all, weight_grad = call(
        functools.partial(total_kernel, sizes),
        [shape((4, quarter, D), BF16), shape((INNER, 4 * D), BF16)],
        2,
        [
            pltpu.VMEM((4, quarter, D), BF16),
            pltpu.VMEM((INNER, 4 * D), BF16),
            pltpu.VMEM((half, 4 * D), BF16),
            pltpu.VMEM((half, 4 * D), BF16),
            [
                pltpu.VMEM((max(x_size - 1, 1), half // x_size, columns), BF16),
                pltpu.VMEM((y_size - 1, half // y_size, columns), BF16),
            ],
            [
                pltpu.VMEM((half // x_size, columns), BF16),
                pltpu.VMEM((half // y_size, columns), BF16),
            ],
            [
                pltpu.VMEM((y_size - 1, last, columns), BF16),
                pltpu.VMEM((max(x_size - 1, 1), last, columns), BF16),
            ],
            pltpu.VMEM((8, 8, D), F32),
            pltpu.VMEM((7, 8, D), F32),
            pltpu.VMEM((8, 8, D), F32),
            [
                pltpu.VMEM((half // x_size, columns), BF16),
                pltpu.VMEM((half // y_size, columns), BF16),
            ],
            pltpu.SemaphoreType.DMA((copies,)),
            pltpu.SemaphoreType.DMA((copies,)),
        ],
        collective_id=1,
        has_side_effects=True,
    )(normed, weight_grad)
    band_mask = call(
        mask_kernel,
        [shape((frames, width), F32)],
        4,
        [pltpu.VMEM((quarter, 2 * D), BF16)],
    )(normed_all, segment, cover, packed)[0]
    qkv_grad = weight_grad[:D].astype(F32)
    out_grad = weight_grad[D:].reshape(INNER // 4, 4, D).transpose(1, 0, 2)
    return band_mask, qkv_grad, out_grad.reshape(INNER, D).astype(F32)


def solution(mesh):
    return jax.shard_map(
        functools.partial(on_device, axis_sizes(mesh.shape["tm"])),
        mesh=mesh,
        in_specs=(
            P("tm", "band"),
            P(),
            P("band", None, None, None),
            P(),
            P(),
            P("band", None, None, None),
            P("tm", "band"),
        ),
        out_specs=(P("tm", "band"), P(), P()),
        check_vma=False,
    )
```

```python
import functools
import math

import jax
import jax.numpy as jnp
import numpy as np
from jax import lax
from jax.experimental import pallas as pl
from jax.experimental.pallas import tpu as pltpu
from jax.sharding import PartitionSpec as P

HEADS = 8
HEAD_DIM = 64
HALF = 32
D = 384
INNER = 512
BANDS = 60
PAD = 64
FEATS = 8
EPSILON = 1e-05
VMEM_BYTES = 50 * 1024 * 1024
BF16 = jnp.bfloat16
F32 = jnp.float32

NN = (((1,), (0,)), ((), ()))
NT = (((1,), (1,)), ((), ()))
TN = (((0,), (0,)), ((), ()))


def dot(left, right, dims=NN):
    return lax.dot_general(left, right, dims, preferred_element_type=F32)


def split_three(values):
    high = values.astype(BF16)
    rest = values - high.astype(F32)
    middle = rest.astype(BF16)
    low = (rest - middle.astype(F32)).astype(BF16)
    return high, middle, low


def iota(shape, dim):
    return lax.broadcasted_iota(jnp.int32, shape, dim)


def segment_masks(assign_ref, first_bin, bin_count):
    rising = assign_ref[:, 0, pl.ds(first_bin, bin_count)].astype(F32).astype(BF16)
    falling = assign_ref[:, 1, pl.ds(first_bin, bin_count)].astype(F32).astype(BF16)
    row, column = iota((PAD, BANDS), 0), iota((PAD, BANDS), 1)
    same = jnp.where(row == column, 1.0, 0.0).astype(BF16)
    last = jnp.where((row == BANDS) & (column == BANDS - 1), 1.0, 0.0).astype(BF16)
    risen = dot(same, rising)
    segments = risen + dot(last, falling)
    bands = risen + dot(same, falling)
    width = bin_count * FEATS
    repeat = jnp.where(
        iota((bin_count, width), 1) // FEATS == iota((bin_count, width), 0), 1.0, 0.0
    ).astype(BF16)
    return dot(segments.astype(BF16), repeat), dot(bands.astype(BF16), repeat)


def pack_weight(weight_ref, packed_ref):
    bin_count = weight_ref.shape[0]
    step = 32
    for first in range(0, bin_count, step):
        for side in range(2):
            block = weight_ref[first : first + step, side].astype(F32)
            packed_ref[first * FEATS : (first + step) * FEATS, side * D : (side + 1) * D] = (
                block.reshape(step * FEATS, D).astype(BF16)
            )


def band_sums(rows_ref, first_row, mask_ref, packed_ref, masked_ref):
    tokens = masked_ref.shape[0]
    mask = mask_ref[...]
    for frame in range(tokens // PAD):
        row = rows_ref[pl.ds(first_row + frame, 1), :].astype(BF16)
        masked_ref[frame * PAD : (frame + 1) * PAD, :] = mask * row
    total = dot(masked_ref[...], packed_ref[...])
    shifted = pltpu.roll(total[:, D:], tokens - 1, 0)
    in_band = iota((tokens, 1), 0) % PAD < BANDS
    return jnp.where(in_band, total[:, :D] + shifted, 0.0).astype(BF16)


def whole_kernel(
    sizes,
    spectrum_ref,
    cotangent_ref,
    assign_ref,
    table_ref,
    split_hbm,
    mask_hbm,
    qkv_hbm,
    out_hbm,
    mask_out,
    qkv_out,
    out_out,
    split_raw,
    mask_raw,
    qkv_ref,
    out_weight_ref,
    split_packed,
    mask_packed,
    spectrum_rows,
    cotangent_rows,
    segment_ref,
    scaled_ref,
    inverse_ref,
    masked_ref,
    energy_ref,
    energies,
    parts,
    from_core,
    to_chip,
    from_chip,
    probs_ref,
    heads_ref,
    attended_ref,
    grad_projected_ref,
    grad_ref,
    normed_all,
    pair_ref,
    gathered,
    core_in,
    pair_sum,
    first_in,
    first_sum,
    second_in,
    second_sum,
    depth_in,
    depth_all,
    second_all,
    load,
    send,
    receive,
):
    x_size, y_high, z_size = sizes
    y_size = y_high * 2
    me_tm, me = lax.axis_index("tm"), lax.axis_index("band")
    chip, core = me // 2, me % 2
    x = me_tm // (y_high * z_size)
    y = (me_tm // z_size) % y_high * 2 + chip
    z = me_tm % z_size
    tokens = masked_ref.shape[0]
    frames = tokens // PAD

    def device(at_x, at_y, at_z, at_core):
        return ((at_x * y_high + at_y // 2) * z_size + at_z, (at_y % 2) * 2 + at_core)

    other_core = (me_tm, chip * 2 + 1 - core)
    other_chip = (me_tm, (1 - chip) * 2 + core)
    diagonal = (me_tm, (1 - chip) * 2 + 1 - core)
    x_peers = [device(lax.rem(x + s, x_size), y, z, core) for s in range(1, x_size)]
    y_peers = [device(x, lax.rem(y + s, y_size), z, core) for s in range(1, y_size)]
    z_peers = [device(x, y, lax.rem(z + s, z_size), core) for s in range(1, z_size)]
    everyone = [other_core, diagonal] + x_peers + y_peers + z_peers
    barrier = pltpu.get_barrier_semaphore()
    for peer in everyone:
        pl.semaphore_signal(barrier, inc=1, device_id=peer, device_id_type=pl.DeviceIdType.MESH)
    loads = []
    for index, (source, target) in enumerate(
        (
            (split_hbm, split_raw),
            (mask_hbm, mask_raw),
            (qkv_hbm, qkv_ref),
            (out_hbm, out_weight_ref),
        )
    ):
        copy = pltpu.make_async_copy(source, target, load.at[index])
        copy.start()
        loads.append(copy)
    next_index = [0]
    started = []

    def begin(source, target, to):
        index = next_index[0]
        next_index[0] += 1
        copy = pltpu.make_async_remote_copy(
            src_ref=source,
            dst_ref=target,
            send_sem=send.at[index],
            recv_sem=receive.at[index],
            device_id=to,
            device_id_type=pl.DeviceIdType.MESH,
        )
        copy.start()
        started.append(copy)
        return copy

    bin_count = split_raw.shape[0]
    first_bin = pl.multiple_of(me * bin_count, bin_count)
    segment_mask, band_mask = segment_masks(assign_ref, first_bin, bin_count)
    segment_ref[...] = segment_mask.astype(BF16)
    inverse = 1.0 / jnp.sum(band_mask, axis=0, keepdims=True)
    inverse_ref[...] = inverse
    scaled_ref[...] = (segment_mask * inverse).astype(BF16)
    spectrum = spectrum_ref[...].astype(F32)
    spectrum_rows[...] = spectrum
    cotangent_rows[...] = cotangent_ref[...].astype(F32)
    band_bf = band_mask.astype(BF16)
    energy = jnp.zeros((spectrum.shape[0], PAD), F32)
    for term in split_three(spectrum * spectrum):
        energy += dot(term, band_bf, NT)
    energy_ref[...] = jnp.zeros_like(energy_ref)
    energy_ref[:, :PAD] = energy

    quarters = [
        (1 - chip) * 2 + 1 - core,
        (1 - chip) * 2 + core,
        chip * 2 + 1 - core,
        me,
    ]
    energy_copies = []
    across = [None, None]
    seconds_in = [None, None]
    for item in range(2):
        loads[item].wait()
        raw, packed = ((split_raw, split_packed), (mask_raw, mask_packed))[item]
        rows_ref, mask_ref = ((spectrum_rows, segment_ref), (cotangent_rows, scaled_ref))[item]
        pack_weight(raw, packed)
        for slot in range(4):
            parts[item, slot] = band_sums(
                rows_ref, quarters[slot] * frames, mask_ref, packed, masked_ref
            )
            if item == 0 and slot == 0:
                pl.semaphore_wait(barrier, len(everyone))
                for index, peer in enumerate((other_core, other_chip, diagonal)):
                    energy_copies.append(begin(energy_ref, energies.at[index], peer))
            if slot == 0:
                first = begin(parts.at[item, 0], from_core.at[item, 0], other_core)
            if slot == 1:
                first.wait_recv()
                to_chip[item] = (
                    parts[item, 1].astype(F32) + from_core[item, 0].astype(F32)
                ).astype(BF16)
                across[item] = begin(to_chip.at[item], from_chip.at[item], other_chip)
            if slot == 2:
                seconds_in[item] = begin(parts.at[item, 2], from_core.at[item, 1], other_core)

    def reduced(item):
        seconds_in[item].wait_recv()
        across[item].wait_recv()
        own = parts[item, 3].astype(F32) + from_core[item, 1].astype(F32)
        return own + from_chip[item].astype(F32)

    for copy in energy_copies:
        copy.wait_recv()
    total_energy = energy_ref[...] + energies[0] + energies[1] + energies[2]
    both = (assign_ref[:, 0, :] + assign_ref[:, 1, :]).astype(F32).astype(BF16)
    bins = both.shape[1]
    band_sizes = FEATS * dot(jnp.ones((8, bins), BF16), both, NT)[:1]
    ratio = total_energy[:, :BANDS] / jnp.maximum(band_sizes, 1.0)
    lane = iota((BANDS, tokens), 1)
    spread = jnp.where(lane % PAD == iota((BANDS, tokens), 0), 1.0, 0.0).astype(BF16)
    rows = total_energy.shape[0]
    energy = jnp.zeros((rows, tokens), F32)
    for term in split_three(ratio):
        energy += dot(term, spread)
    mine = iota((rows, tokens), 0) == me * frames + iota((rows, tokens), 1) // PAD
    energy = jnp.sum(jnp.where(mine, energy, 0.0), axis=0, keepdims=True)
    in_band = iota((1, tokens), 1) % PAD < BANDS
    loads[2].wait()
    loads[3].wait()

    hidden_in = (jnp.transpose(reduced(0)) * lax.rsqrt(energy + EPSILON)).astype(BF16)
    hidden_in = hidden_in.astype(F32)
    normed_in = (
        hidden_in
        * lax.rsqrt(jnp.mean(hidden_in * hidden_in, axis=0, keepdims=True) + EPSILON)
    ).astype(BF16)
    projected = dot(qkv_ref[...], normed_in, TN)
    cos, sin = table_ref[:HALF, :], table_ref[HALF:, :]
    scale = HEAD_DIM**-0.5
    key_lane, query_lane = iota((tokens, tokens), 0), iota((tokens, tokens), 1)
    allowed = (key_lane // PAD == query_lane // PAD) & (key_lane % PAD < BANDS)
    bias = jnp.where(allowed, 0.0, -1e30)
    for head in range(HEADS):
        for part in range(2):
            base = part * INNER + head * HEAD_DIM
            front = projected[base : base + HALF]
            back = projected[base + HALF : base + HEAD_DIM]
            factor = scale if part == 0 else 1.0
            heads_ref[base : base + HALF, :] = ((front * cos - back * sin) * factor).astype(BF16)
            heads_ref[base + HALF : base + HEAD_DIM, :] = (
                (front * sin + back * cos) * factor
            ).astype(BF16)
    heads_ref[2 * INNER :, :] = projected[2 * INNER :].astype(BF16)

    def part_of(part, head):
        base = part * INNER + head * HEAD_DIM
        return heads_ref[base : base + HEAD_DIM, :]

    for head in range(HEADS):
        scores = dot(part_of(1, head), part_of(0, head), TN) + bias
        powers = jnp.exp(scores - jnp.max(scores, axis=0, keepdims=True))
        probs = powers / jnp.sum(powers, axis=0, keepdims=True)
        probs_ref[head] = probs
        attended_ref[head * HEAD_DIM : (head + 1) * HEAD_DIM, :] = dot(
            part_of(2, head), probs.astype(BF16)
        ).astype(BF16)
    mixed = dot(out_weight_ref[...], attended_ref[...], TN)
    hidden_out = (hidden_in + mixed).astype(BF16).astype(F32)
    inverse = lax.rsqrt(jnp.mean(hidden_out * hidden_out, axis=0, keepdims=True) + EPSILON)
    normed_out = jnp.where(in_band, hidden_out * inverse, 0.0)
    normed_all[me] = jnp.transpose(normed_out).astype(BF16)
    to_chip_rows = begin(normed_all.at[me], normed_all.at[me], other_chip)
    to_core_rows = begin(normed_all.at[me], normed_all.at[me], other_core)

    upstream = jnp.transpose(reduced(1))
    inner = jnp.mean(upstream * hidden_out, axis=0, keepdims=True)
    grad_hidden = (
        inverse * upstream - hidden_out * (inverse * inverse * inverse) * inner
    ).astype(BF16)
    grad_attended = dot(out_weight_ref[...], grad_hidden).astype(BF16)
    out_grad = dot(attended_ref[...], grad_hidden, NT).astype(BF16)
    quarter = INNER // 4
    for block in range(4):
        grad_ref[D:, block * D : (block + 1) * D] = out_grad[
            block * quarter : (block + 1) * quarter
        ]
    for head in range(HEADS):
        probs = probs_ref[head]
        grad_head = grad_attended[head * HEAD_DIM : (head + 1) * HEAD_DIM]
        grad_probs = dot(part_of(2, head), grad_head, TN)
        row_sum = jnp.sum(grad_probs * probs, axis=0, keepdims=True)
        grad_scores = (probs * (grad_probs - row_sum)).astype(BF16)
        grad_values = dot(grad_head, probs.astype(BF16), NT)
        grad_queries = dot(part_of(1, head), grad_scores) * scale
        grad_keys = dot(part_of(0, head), grad_scores, NT)
        for part, grad in ((0, grad_queries), (1, grad_keys)):
            base = part * INNER + head * HEAD_DIM
            front, back = grad[:HALF], grad[HALF:]
            grad_projected_ref[base : base + HALF, :] = (front * cos + back * sin).astype(BF16)
            grad_projected_ref[base + HALF : base + HEAD_DIM, :] = (
                back * cos - front * sin
            ).astype(BF16)
        base = 2 * INNER + head * HEAD_DIM
        grad_projected_ref[base : base + HEAD_DIM, :] = grad_values.astype(BF16)
    grad_ref[:D, :] = dot(normed_in, grad_projected_ref[...], NT).astype(BF16)

    def mask_rows(quarter):
        normed = normed_all[quarter]
        pair_ref[:, :D] = normed
        pair_ref[:, D:] = pltpu.roll(normed.astype(F32), 1, 0).astype(BF16)
        estimate = dot(pair_ref[...], mask_packed[...], NT)
        mask = segment_ref[...].astype(F32)
        for frame in range(frames):
            block = estimate[frame * PAD : (frame + 1) * PAD]
            mask_out[pl.ds(quarter * frames + frame, 1), :] = (
                jnp.sum(block * mask, axis=0, keepdims=True) * inverse_ref[...]
            )

    half = grad_ref.shape[0] // 2
    columns = grad_ref.shape[1] // 2
    left, right = pl.ds(0, columns), pl.ds(columns, columns)
    pair_copy = begin(
        grad_ref.at[pl.ds(pl.multiple_of((1 - core) * half, half), half), :], core_in, other_core
    )
    to_chip_rows.wait_recv()
    chip_rows = normed_all.at[(1 - chip) * 2 + core]
    onward = begin(chip_rows, chip_rows, other_core)
    mask_rows(me)
    pair_copy.wait_recv()
    own = pl.ds(pl.multiple_of(core * half, half), half)
    pair_sum[...] = (grad_ref[own, :].astype(F32) + core_in[...].astype(F32)).astype(BF16)

    axes = ((x, x_size, x_peers), (y, y_size, y_peers))
    counts = [half // x_size, half // y_size]
    firsts = ([], [])
    for step in range(max(x_size, y_size) - 1):
        for part in range(2):
            at, size, peers = axes[part]
            if step < size - 1:
                count = counts[part]
                there = pl.ds(pl.multiple_of(lax.rem(at + step + 1, size) * count, count), count)
                firsts[part].append(
                    begin(
                        pair_sum.at[there, (left, right)[part]],
                        first_in[part].at[step],
                        peers[step],
                    )
                )
    to_core_rows.wait_recv()
    mask_rows(chip * 2 + 1 - core)
    for part in range(2):
        at, size, peers = axes[part]
        count = counts[part]
        here = pl.ds(pl.multiple_of(at * count, count), count)
        total = pair_sum[here, (left, right)[part]].astype(F32)
        for step in range(size - 1):
            firsts[part][step].wait_recv()
            total += first_in[part][step].astype(F32)
        first_sum[part][...] = total.astype(BF16)

    last_rows = half // (x_size * y_size)
    seconds = ([], [])
    for part in range(2):
        at, size, peers = axes[1 - part]
        for step in range(size - 1):
            there = pl.ds(
                pl.multiple_of(lax.rem(at + step + 1, size) * last_rows, last_rows), last_rows
            )
            seconds[part].append(
                begin(first_sum[part].at[there, :], second_in[part].at[step], peers[step])
            )
    mask_rows((1 - chip) * 2 + core)
    chunk_rows, chunk_columns = 8, columns // 2
    for part in range(2):
        at, size, peers = axes[1 - part]
        here = pl.ds(pl.multiple_of(at * last_rows, last_rows), last_rows)
        total = first_sum[part][here, :].astype(F32)
        for step in range(size - 1):
            seconds[part][step].wait_recv()
            total += second_in[part][step].astype(F32)
        if z_size == 1:
            second_all[part][here, :] = total.astype(BF16)
        else:
            for block in range(4):
                r, c = block // 2 * chunk_rows, block % 2 * chunk_columns
                second_sum[part * 4 + block] = total[r : r + chunk_rows, c : c + chunk_columns]

    if z_size > 1:
        depths = [
            begin(second_sum.at[lax.rem(z + s, z_size)], depth_in.at[s - 1], z_peers[s - 1])
            for s in range(1, z_size)
        ]
    onward.wait_recv()
    mask_rows((1 - chip) * 2 + 1 - core)
    if z_size > 1:
        total = second_sum[z]
        for step in range(z_size - 1):
            depths[step].wait_recv()
            total += depth_in[step]
        depth_all[z] = total
        backs = [begin(depth_all.at[z], depth_all.at[z], peer) for peer in z_peers]
        for copy in backs:
            copy.wait_recv()
        for part in range(2):
            at = axes[1 - part][0]
            here = pl.ds(pl.multiple_of(at * last_rows, last_rows), last_rows)
            rows_of = []
            for high in range(2):
                rows_of.append(
                    jnp.concatenate(
                        [depth_all[part * 4 + high * 2], depth_all[part * 4 + high * 2 + 1]], axis=1
                    )
                )
            second_all[part][here, :] = jnp.concatenate(rows_of, axis=0).astype(BF16)

    backs = ([], [])
    for part in range(2):
        at, size, peers = axes[1 - part]
        here = pl.ds(pl.multiple_of(at * last_rows, last_rows), last_rows)
        for peer in peers:
            backs[part].append(
                begin(second_all[part].at[here, :], second_all[part].at[here, :], peer)
            )
    spread = ([], [])
    mirrored = []
    base = core * half
    for part in range(2):
        for copy in backs[part]:
            copy.wait_recv()
        at, size, peers = axes[part]
        count = counts[part]
        here = pl.ds(pl.multiple_of(base + at * count, count), count)
        target = gathered.at[here, (left, right)[part]]
        for peer in peers:
            spread[part].append(begin(second_all[part], target, peer))
        gathered[here, (left, right)[part]] = second_all[part][...]
        mirrored.append(begin(second_all[part], target, other_core))
    for step in range(max(x_size, y_size) - 1):
        for part in range(2):
            at, size, peers = axes[part]
            if step < size - 1:
                count = counts[part]
                spread[part][step].wait_recv()
                origin = lax.rem(at + size - step - 1, size)
                here = pl.ds(pl.multiple_of(base + origin * count, count), count)
                block = gathered.at[here, (left, right)[part]]
                mirrored.append(begin(block, block, other_core))
    for copy in mirrored:
        copy.wait_recv()
    qkv_out[...] = gathered[:D, :].astype(F32)
    for block in range(4):
        out_out[block * quarter : (block + 1) * quarter, :] = gathered[
            D:, block * D : (block + 1) * D
        ].astype(F32)
    for copy in started:
        copy.wait_send()


def rotary_table(tokens):
    position = (np.arange(tokens) % PAD).astype(np.float64)[None, :]
    frequency = np.exp(-math.log(10000.0) * np.arange(HALF) / HALF)[:, None]
    angles = position * frequency
    return np.concatenate([np.cos(angles), np.sin(angles)], axis=0).astype(np.float32)


def axis_sizes(tm_size):
    return {64: (4, 2, 8), 8: (4, 2, 1), 4: (4, 1, 1), 2: (2, 1, 1), 1: (1, 1, 1)}[tm_size]


def on_device(
    sizes, spectrum, band_assign, split_weight, qkv_weight, out_weight, mask_weight, mask_cotangent
):
    frames, width = spectrum.shape
    tokens = frames // 4 * PAD
    x_size, y_high, z_size = sizes
    y_size = 2 * y_high
    half, columns = INNER // 2, 2 * D
    last = half // (x_size * y_size)
    copies = 72

    def vmem(*shape, dtype=BF16):
        return pltpu.VMEM(shape, dtype)

    inside = pl.BlockSpec(memory_space=pltpu.VMEM)
    anywhere = pl.BlockSpec(memory_space=pl.ANY)
    assign = jnp.transpose(band_assign, (2, 0, 1))
    return pl.pallas_call(
        functools.partial(whole_kernel, sizes),
        out_shape=[
            jax.ShapeDtypeStruct((frames, width), F32),
            jax.ShapeDtypeStruct(qkv_weight.shape, F32),
            jax.ShapeDtypeStruct(out_weight.shape, F32),
        ],
        in_specs=[inside] * 4 + [anywhere] * 4,
        out_specs=[inside] * 3,
        scratch_shapes=[
            vmem(*split_weight.shape),
            vmem(*mask_weight.shape),
            vmem(*qkv_weight.shape),
            vmem(*out_weight.shape),
            vmem(width, 2 * D),
            vmem(width, 2 * D),
            vmem(frames, width, dtype=F32),
            vmem(frames, width, dtype=F32),
            vmem(PAD, width),
            vmem(PAD, width),
            vmem(1, width, dtype=F32),
            vmem(tokens, width),
            vmem(frames, 128, dtype=F32),
            vmem(3, frames, 128, dtype=F32),
            vmem(2, 4, tokens, D),
            vmem(2, 2, tokens, D),
            vmem(2, tokens, D),
            vmem(2, tokens, D),
            vmem(HEADS, tokens, tokens, dtype=F32),
            vmem(3 * INNER, tokens),
            vmem(INNER, tokens),
            vmem(3 * INNER, tokens),
            vmem(INNER, 4 * D),
            vmem(4, tokens, D),
            vmem(tokens, 2 * D),
            vmem(INNER, 4 * D),
            vmem(half, 4 * D),
            vmem(half, 4 * D),
            [
                vmem(max(x_size - 1, 1), half // x_size, columns),
                vmem(y_size - 1, half // y_size, columns),
            ],
            [vmem(half // x_size, columns), vmem(half // y_size, columns)],
            [vmem(y_size - 1, last, columns), vmem(max(x_size - 1, 1), last, columns)],
            vmem(8, 8, D, dtype=F32),
            vmem(7, 8, D, dtype=F32),
            vmem(8, 8, D, dtype=F32),
            [vmem(half // x_size, columns), vmem(half // y_size, columns)],
            pltpu.SemaphoreType.DMA((4,)),
            pltpu.SemaphoreType.DMA((copies,)),
            pltpu.SemaphoreType.DMA((copies,)),
        ],
        compiler_params=pltpu.CompilerParams(
            vmem_limit_bytes=VMEM_BYTES, collective_id=0, has_side_effects=True
        ),
    )(
        spectrum,
        mask_cotangent,
        assign,
        jnp.asarray(rotary_table(tokens)),
        split_weight,
        mask_weight,
        qkv_weight,
        out_weight,
    )


def solution(mesh):
    return jax.shard_map(
        functools.partial(on_device, axis_sizes(mesh.shape["tm"])),
        mesh=mesh,
        in_specs=(
            P("tm", "band"),
            P(),
            P("band", None, None, None),
            P(),
            P(),
            P("band", None, None, None),
            P("tm", "band"),
        ),
        out_specs=(P("tm", "band"), P(), P()),
        check_vma=False,
    )
```

```python
import functools
import math

import jax
import jax.numpy as jnp
import numpy as np
from jax import lax
from jax.experimental import pallas as pl
from jax.experimental.pallas import tpu as pltpu
from jax.sharding import PartitionSpec as P

HEADS = 8
HEAD_DIM = 64
HALF = 32
D = 384
INNER = 512
BANDS = 60
PAD = 64
FEATS = 8
EPSILON = 1e-05
VMEM_BYTES = 50 * 1024 * 1024
BF16 = jnp.bfloat16
F32 = jnp.float32

NN = (((1,), (0,)), ((), ()))
NT = (((1,), (1,)), ((), ()))
TN = (((0,), (0,)), ((), ()))


def dot(left, right, dims=NN):
    return lax.dot_general(left, right, dims, preferred_element_type=F32)


def split_three(values):
    high = values.astype(BF16)
    rest = values - high.astype(F32)
    middle = rest.astype(BF16)
    low = (rest - middle.astype(F32)).astype(BF16)
    return high, middle, low


def iota(shape, dim):
    return lax.broadcasted_iota(jnp.int32, shape, dim)


def segment_masks(assign_ref, first_bin, bin_count):
    rising = assign_ref[:, 0, pl.ds(first_bin, bin_count)].astype(F32).astype(BF16)
    falling = assign_ref[:, 1, pl.ds(first_bin, bin_count)].astype(F32).astype(BF16)
    row, column = iota((PAD, BANDS), 0), iota((PAD, BANDS), 1)
    same = jnp.where(row == column, 1.0, 0.0).astype(BF16)
    last = jnp.where((row == BANDS) & (column == BANDS - 1), 1.0, 0.0).astype(BF16)
    risen = dot(same, rising)
    segments = risen + dot(last, falling)
    bands = risen + dot(same, falling)
    width = bin_count * FEATS
    repeat = jnp.where(
        iota((bin_count, width), 1) // FEATS == iota((bin_count, width), 0), 1.0, 0.0
    ).astype(BF16)
    return dot(segments.astype(BF16), repeat), bands.astype(BF16), repeat


def pack_weight(weight_ref, packed_ref):
    bin_count = weight_ref.shape[0]
    step = 32
    for first in range(0, bin_count, step):
        for side in range(2):
            block = weight_ref[first : first + step, side].astype(F32)
            packed_ref[first * FEATS : (first + step) * FEATS, side * D : (side + 1) * D] = (
                block.reshape(step * FEATS, D).astype(BF16)
            )


def band_sums(rows_ref, first_row, mask_ref, packed_ref, masked_ref):
    tokens = masked_ref.shape[0]
    mask = mask_ref[...]
    for frame in range(tokens // PAD):
        row = rows_ref[pl.ds(first_row + frame, 1), :].astype(BF16)
        masked_ref[frame * PAD : (frame + 1) * PAD, :] = mask * row
    total = dot(masked_ref[...], packed_ref[...])
    shifted = pltpu.roll(total[:, D:], tokens - 1, 0)
    in_band = iota((tokens, 1), 0) % PAD < BANDS
    return jnp.where(in_band, total[:, :D] + shifted, 0.0).astype(BF16)


def whole_kernel(
    sizes,
    spectrum_hbm,
    cotangent_hbm,
    assign_hbm,
    table_hbm,
    split_hbm,
    mask_hbm,
    qkv_hbm,
    out_hbm,
    mask_out,
    gathered,
    spectrum_ref,
    cotangent_ref,
    assign_ref,
    table_ref,
    split_raw,
    mask_raw,
    qkv_ref,
    out_weight_ref,
    split_packed,
    mask_packed,
    spectrum_rows,
    cotangent_rows,
    segment_ref,
    scaled_ref,
    inverse_ref,
    masked_ref,
    energy_ref,
    energies,
    parts,
    from_core,
    to_chip,
    from_chip,
    probs_ref,
    heads_ref,
    attended_ref,
    grad_projected_ref,
    grad_ref,
    normed_all,
    pair_ref,
    core_in,
    pair_sum,
    first_in,
    first_sum,
    second_in,
    second_sum,
    depth_in,
    depth_all,
    second_all,
    load,
    send,
    receive,
):
    x_size, y_high, z_size = sizes
    y_size = y_high * 2
    me_tm, me = lax.axis_index("tm"), lax.axis_index("band")
    chip, core = me // 2, me % 2
    x = me_tm // (y_high * z_size)
    y = (me_tm // z_size) % y_high * 2 + chip
    z = me_tm % z_size
    tokens = masked_ref.shape[0]
    frames = tokens // PAD

    def device(at_x, at_y, at_z, at_core):
        return ((at_x * y_high + at_y // 2) * z_size + at_z, (at_y % 2) * 2 + at_core)

    other_core = (me_tm, chip * 2 + 1 - core)
    other_chip = (me_tm, (1 - chip) * 2 + core)
    diagonal = (me_tm, (1 - chip) * 2 + 1 - core)
    x_peers = [device(lax.rem(x + s, x_size), y, z, core) for s in range(1, x_size)]
    y_peers = [device(x, lax.rem(y + s, y_size), z, core) for s in range(1, y_size)]
    z_peers = [device(x, y, lax.rem(z + s, z_size), core) for s in range(1, z_size)]
    everyone = [other_core, diagonal] + x_peers + y_peers + z_peers
    barrier = pltpu.get_barrier_semaphore()
    for peer in everyone:
        pl.semaphore_signal(barrier, inc=1, device_id=peer, device_id_type=pl.DeviceIdType.MESH)
    loads = []
    for index, (source, target) in enumerate(
        (
            (assign_hbm, assign_ref),
            (spectrum_hbm, spectrum_ref),
            (split_hbm, split_raw),
            (cotangent_hbm, cotangent_ref),
            (mask_hbm, mask_raw),
            (qkv_hbm, qkv_ref),
            (out_hbm, out_weight_ref),
            (table_hbm, table_ref),
        )
    ):
        copy = pltpu.make_async_copy(source, target, load.at[index])
        copy.start()
        loads.append(copy)
    next_index = [0]
    started = []

    def begin(source, target, to):
        index = next_index[0]
        next_index[0] += 1
        copy = pltpu.make_async_remote_copy(
            src_ref=source,
            dst_ref=target,
            send_sem=send.at[index],
            recv_sem=receive.at[index],
            device_id=to,
            device_id_type=pl.DeviceIdType.MESH,
        )
        copy.start()
        started.append(copy)
        return copy

    def drain():
        while started:
            started.pop(0).wait_send()

    bin_count = split_raw.shape[0]
    first_bin = pl.multiple_of(me * bin_count, bin_count)
    loads[0].wait()
    segment_mask, bands, repeat = segment_masks(assign_ref, first_bin, bin_count)
    segment_ref[...] = segment_mask.astype(BF16)
    loads[1].wait()
    spectrum = spectrum_ref[...].astype(F32)
    spectrum_rows[...] = spectrum

    quarters = [
        (1 - chip) * 2 + 1 - core,
        (1 - chip) * 2 + core,
        chip * 2 + 1 - core,
        me,
    ]
    energy_copies = []
    across = [None, None]
    seconds_in = [None, None]
    for item in range(2):
        loads[2 + 2 * item].wait()
        raw, packed = ((split_raw, split_packed), (mask_raw, mask_packed))[item]
        rows_ref, mask_ref = ((spectrum_rows, segment_ref), (cotangent_rows, scaled_ref))[item]
        pack_weight(raw, packed)
        for slot in range(4):
            parts[item, slot] = band_sums(
                rows_ref, quarters[slot] * frames, mask_ref, packed, masked_ref
            )
            if slot == 0:
                if item == 0:
                    pl.semaphore_wait(barrier, len(everyone))
                first = begin(parts.at[item, 0], from_core.at[item, 0], other_core)
                if item == 0:
                    band_mask = dot(bands, repeat)
                    inverse = 1.0 / jnp.sum(band_mask, axis=0, keepdims=True)
                    inverse_ref[...] = inverse
                    scaled_ref[...] = (segment_mask * inverse).astype(BF16)
                    loads[3].wait()
                    cotangent_rows[...] = cotangent_ref[...].astype(F32)
                    band_bf = band_mask.astype(BF16)
                    energy = jnp.zeros((spectrum.shape[0], PAD), F32)
                    for term in split_three(spectrum * spectrum):
                        energy += dot(term, band_bf, NT)
                    energy_ref[...] = jnp.zeros_like(energy_ref)
                    energy_ref[:, :PAD] = energy
                    for index, peer in enumerate((other_core, other_chip, diagonal)):
                        energy_copies.append(begin(energy_ref, energies.at[index], peer))
            if slot == 1:
                first.wait_recv()
                to_chip[item] = (
                    parts[item, 1].astype(F32) + from_core[item, 0].astype(F32)
                ).astype(BF16)
                across[item] = begin(to_chip.at[item], from_chip.at[item], other_chip)
            if slot == 2:
                seconds_in[item] = begin(parts.at[item, 2], from_core.at[item, 1], other_core)

    def reduced(item):
        seconds_in[item].wait_recv()
        across[item].wait_recv()
        own = parts[item, 3].astype(F32) + from_core[item, 1].astype(F32)
        return own + from_chip[item].astype(F32)

    for copy in energy_copies:
        copy.wait_recv()
    total_energy = energy_ref[...] + energies[0] + energies[1] + energies[2]
    both = (assign_ref[:, 0, :] + assign_ref[:, 1, :]).astype(F32).astype(BF16)
    bins = both.shape[1]
    band_sizes = FEATS * dot(jnp.ones((8, bins), BF16), both, NT)[:1]
    ratio = total_energy[:, :BANDS] / jnp.maximum(band_sizes, 1.0)
    lane = iota((BANDS, tokens), 1)
    spread = jnp.where(lane % PAD == iota((BANDS, tokens), 0), 1.0, 0.0).astype(BF16)
    rows = total_energy.shape[0]
    energy = jnp.zeros((rows, tokens), F32)
    for term in split_three(ratio):
        energy += dot(term, spread)
    mine = iota((rows, tokens), 0) == me * frames + iota((rows, tokens), 1) // PAD
    energy = jnp.sum(jnp.where(mine, energy, 0.0), axis=0, keepdims=True)
    in_band = iota((1, tokens), 1) % PAD < BANDS
    for copy in loads[5:]:
        copy.wait()

    hidden_in = (jnp.transpose(reduced(0)) * lax.rsqrt(energy + EPSILON)).astype(BF16)
    hidden_in = hidden_in.astype(F32)
    normed_in = (
        hidden_in
        * lax.rsqrt(jnp.mean(hidden_in * hidden_in, axis=0, keepdims=True) + EPSILON)
    ).astype(BF16)
    projected = dot(qkv_ref[...], normed_in, TN)
    cos, sin = table_ref[:HALF, :], table_ref[HALF:, :]
    scale = HEAD_DIM**-0.5
    key_lane, query_lane = iota((tokens, tokens), 0), iota((tokens, tokens), 1)
    allowed = (key_lane // PAD == query_lane // PAD) & (key_lane % PAD < BANDS)
    bias = jnp.where(allowed, 0.0, -1e30)
    for head in range(HEADS):
        for part in range(2):
            base = part * INNER + head * HEAD_DIM
            front = projected[base : base + HALF]
            back = projected[base + HALF : base + HEAD_DIM]
            factor = scale if part == 0 else 1.0
            heads_ref[base : base + HALF, :] = ((front * cos - back * sin) * factor).astype(BF16)
            heads_ref[base + HALF : base + HEAD_DIM, :] = (
                (front * sin + back * cos) * factor
            ).astype(BF16)
    heads_ref[2 * INNER :, :] = projected[2 * INNER :].astype(BF16)

    def part_of(part, head):
        base = part * INNER + head * HEAD_DIM
        return heads_ref[base : base + HEAD_DIM, :]

    for head in range(HEADS):
        scores = dot(part_of(1, head), part_of(0, head), TN) + bias
        powers = jnp.exp(scores - jnp.max(scores, axis=0, keepdims=True))
        probs = powers / jnp.sum(powers, axis=0, keepdims=True)
        probs_ref[head] = probs
        attended_ref[head * HEAD_DIM : (head + 1) * HEAD_DIM, :] = dot(
            part_of(2, head), probs.astype(BF16)
        ).astype(BF16)
    mixed = dot(out_weight_ref[...], attended_ref[...], TN)
    hidden_out = (hidden_in + mixed).astype(BF16).astype(F32)
    inverse = lax.rsqrt(jnp.mean(hidden_out * hidden_out, axis=0, keepdims=True) + EPSILON)
    normed_out = jnp.where(in_band, hidden_out * inverse, 0.0)
    normed_all[me] = jnp.transpose(normed_out).astype(BF16)
    to_chip_rows = begin(normed_all.at[me], normed_all.at[me], other_chip)
    to_core_rows = begin(normed_all.at[me], normed_all.at[me], other_core)

    upstream = jnp.transpose(reduced(1))
    inner = jnp.mean(upstream * hidden_out, axis=0, keepdims=True)
    grad_hidden = (
        inverse * upstream - hidden_out * (inverse * inverse * inverse) * inner
    ).astype(BF16)
    grad_attended = dot(out_weight_ref[...], grad_hidden).astype(BF16)
    out_grad = dot(attended_ref[...], grad_hidden, NT).astype(BF16)
    quarter = INNER // 4
    for block in range(4):
        grad_ref[D:, block * D : (block + 1) * D] = out_grad[
            block * quarter : (block + 1) * quarter
        ]
    for head in range(HEADS):
        probs = probs_ref[head]
        grad_head = grad_attended[head * HEAD_DIM : (head + 1) * HEAD_DIM]
        grad_probs = dot(part_of(2, head), grad_head, TN)
        row_sum = jnp.sum(grad_probs * probs, axis=0, keepdims=True)
        grad_scores = (probs * (grad_probs - row_sum)).astype(BF16)
        grad_values = dot(grad_head, probs.astype(BF16), NT)
        grad_queries = dot(part_of(1, head), grad_scores) * scale
        grad_keys = dot(part_of(0, head), grad_scores, NT)
        for part, grad in ((0, grad_queries), (1, grad_keys)):
            base = part * INNER + head * HEAD_DIM
            front, back = grad[:HALF], grad[HALF:]
            grad_projected_ref[base : base + HALF, :] = (front * cos + back * sin).astype(BF16)
            grad_projected_ref[base + HALF : base + HEAD_DIM, :] = (
                back * cos - front * sin
            ).astype(BF16)
        base = 2 * INNER + head * HEAD_DIM
        grad_projected_ref[base : base + HEAD_DIM, :] = grad_values.astype(BF16)
    grad_ref[:D, :] = dot(normed_in, grad_projected_ref[...], NT).astype(BF16)

    def mask_rows(quarter):
        normed = normed_all[quarter]
        pair_ref[:, :D] = normed
        pair_ref[:, D:] = pltpu.roll(normed.astype(F32), 1, 0).astype(BF16)
        estimate = dot(pair_ref[...], mask_packed[...], NT)
        mask = segment_ref[...].astype(F32)
        for frame in range(frames):
            block = estimate[frame * PAD : (frame + 1) * PAD]
            mask_out[pl.ds(quarter * frames + frame, 1), :] = (
                jnp.sum(block * mask, axis=0, keepdims=True) * inverse_ref[...]
            )

    half = grad_ref.shape[0] // 2
    columns = grad_ref.shape[1] // 2
    pair_copy = begin(
        grad_ref.at[pl.ds(pl.multiple_of((1 - core) * half, half), half), :], core_in, other_core
    )
    mask_rows(me)
    pair_copy.wait_recv()
    own = pl.ds(pl.multiple_of(core * half, half), half)
    both_cores = (grad_ref[own, :].astype(F32) + core_in[...].astype(F32)).astype(BF16)
    pair_sum[0] = both_cores[:, :columns]
    pair_sum[1] = both_cores[:, columns:]

    axes = ((x, x_size, x_peers), (y, y_size, y_peers))
    counts = [half // x_size, half // y_size]
    firsts = ([], [])
    for step in range(max(x_size, y_size) - 1):
        for part in range(2):
            at, size, peers = axes[part]
            if step < size - 1:
                count = counts[part]
                there = pl.ds(pl.multiple_of(lax.rem(at + step + 1, size) * count, count), count)
                firsts[part].append(
                    begin(
                        pair_sum.at[part, there, :],
                        first_in[part].at[step],
                        peers[step],
                    )
                )
    to_core_rows.wait_recv()
    mask_rows(chip * 2 + 1 - core)
    to_chip_rows.wait_recv()
    chip_rows = normed_all.at[(1 - chip) * 2 + core]
    onward = begin(chip_rows, chip_rows, other_core)
    for part in range(2):
        at, size, peers = axes[part]
        count = counts[part]
        here = pl.ds(pl.multiple_of(at * count, count), count)
        total = pair_sum[part, here, :].astype(F32)
        for step in range(size - 1):
            firsts[part][step].wait_recv()
            total += first_in[part][step].astype(F32)
        first_sum[part][...] = total.astype(BF16)

    last_rows = half // (x_size * y_size)
    seconds = ([], [])
    for part in range(2):
        at, size, peers = axes[1 - part]
        for step in range(size - 1):
            there = pl.ds(
                pl.multiple_of(lax.rem(at + step + 1, size) * last_rows, last_rows), last_rows
            )
            seconds[part].append(
                begin(first_sum[part].at[there, :], second_in[part].at[step], peers[step])
            )
    mask_rows((1 - chip) * 2 + core)
    chunk_rows, chunk_columns = 8, columns // 2
    for part in range(2):
        at, size, peers = axes[1 - part]
        here = pl.ds(pl.multiple_of(at * last_rows, last_rows), last_rows)
        total = first_sum[part][here, :].astype(F32)
        for step in range(size - 1):
            seconds[part][step].wait_recv()
            total += second_in[part][step].astype(F32)
        if z_size == 1:
            second_all[part][here, :] = total.astype(BF16)
        else:
            for block in range(4):
                r, c = block // 2 * chunk_rows, block % 2 * chunk_columns
                second_sum[part * 4 + block] = total[r : r + chunk_rows, c : c + chunk_columns]

    if z_size > 1:
        depths = [
            begin(second_sum.at[lax.rem(z + s, z_size)], depth_in.at[s - 1], z_peers[s - 1])
            for s in range(1, z_size)
        ]
    onward.wait_recv()
    mask_rows((1 - chip) * 2 + 1 - core)
    drain()
    if z_size > 1:
        total = second_sum[z]
        for step in range(z_size - 1):
            depths[step].wait_recv()
            total += depth_in[step]
        depth_all[z] = total
        backs = [begin(depth_all.at[z], depth_all.at[z], peer) for peer in z_peers]
        for copy in backs:
            copy.wait_recv()
        for part in range(2):
            at = axes[1 - part][0]
            here = pl.ds(pl.multiple_of(at * last_rows, last_rows), last_rows)
            rows_of = []
            for high in range(2):
                rows_of.append(
                    jnp.concatenate(
                        [depth_all[part * 4 + high * 2], depth_all[part * 4 + high * 2 + 1]], axis=1
                    )
                )
            second_all[part][here, :] = jnp.concatenate(rows_of, axis=0).astype(BF16)

    backs = ([], [])
    for part in range(2):
        at, size, peers = axes[1 - part]
        here = pl.ds(pl.multiple_of(at * last_rows, last_rows), last_rows)
        for peer in peers:
            backs[part].append(
                begin(second_all[part].at[here, :], second_all[part].at[here, :], peer)
            )
    spread = ([], [])
    for part in range(2):
        for copy in backs[part]:
            copy.wait_recv()
        at, size, peers = axes[part]
        count = counts[part]
        here = pl.ds(pl.multiple_of(at * count, count), count)
        target = gathered.at[part, core, here, :]
        for peer in peers:
            spread[part].append(begin(second_all[part], target, peer))
        gathered[part, core, here, :] = second_all[part][...]
    mirrored = []
    for part in range(2):
        for copy in spread[part]:
            copy.wait_recv()
        whole = gathered.at[part, core]
        mirrored.append(begin(whole, whole, other_core))
    for copy in mirrored:
        copy.wait_recv()
    drain()


def store_kernel(gathered_ref, rows_ref, mask_hbm, qkv_hbm, out_hbm, qkv_ref, out_ref, store):
    copies = [pltpu.make_async_copy(rows_ref, mask_hbm, store.at[0])]
    copies[0].start()
    columns = gathered_ref.shape[3]
    quarter = INNER // 4
    for block in range(3):
        here = slice(block * quarter, (block + 1) * quarter)
        there = slice(block % 2 * quarter, (block % 2 + 1) * quarter)
        for part in range(2):
            qkv_ref[here, part * columns : (part + 1) * columns] = gathered_ref[
                part, block // 2, there, :
            ].astype(F32)
        copies.append(
            pltpu.make_async_copy(qkv_ref.at[here, :], qkv_hbm.at[here, :], store.at[1 + block])
        )
        copies[-1].start()
    for block in range(4):
        out_ref[block * quarter : (block + 1) * quarter, :] = gathered_ref[
            block // 2, 1, quarter:, block % 2 * D : (block % 2 + 1) * D
        ].astype(F32)
    copies.append(pltpu.make_async_copy(out_ref, out_hbm, store.at[4]))
    copies[-1].start()
    for copy in copies:
        copy.wait()


def rotary_table(tokens):
    position = (np.arange(tokens) % PAD).astype(np.float64)[None, :]
    frequency = np.exp(-math.log(10000.0) * np.arange(HALF) / HALF)[:, None]
    angles = position * frequency
    return np.concatenate([np.cos(angles), np.sin(angles)], axis=0).astype(np.float32)


def axis_sizes(tm_size):
    return {64: (4, 2, 8), 8: (4, 2, 1), 4: (4, 1, 1), 2: (2, 1, 1), 1: (1, 1, 1)}[tm_size]


def on_device(
    sizes, spectrum, band_assign, split_weight, qkv_weight, out_weight, mask_weight, mask_cotangent
):
    frames, width = spectrum.shape
    tokens = frames // 4 * PAD
    x_size, y_high, z_size = sizes
    y_size = 2 * y_high
    half, columns = INNER // 2, 2 * D
    last = half // (x_size * y_size)
    copies = 72

    def vmem(*shape, dtype=BF16):
        return pltpu.VMEM(shape, dtype)

    inside = pl.BlockSpec(memory_space=pltpu.VMEM)
    outside = pl.BlockSpec(memory_space=pltpu.HBM)
    assign = jnp.transpose(band_assign, (2, 0, 1))
    rows, gathered = pl.pallas_call(
        functools.partial(whole_kernel, sizes),
        out_shape=[
            jax.ShapeDtypeStruct((frames, width), F32),
            jax.ShapeDtypeStruct((2, 2, half, columns), BF16),
        ],
        in_specs=[outside] * 8,
        out_specs=[inside] * 2,
        scratch_shapes=[
            vmem(frames, width),
            vmem(frames, width),
            vmem(*assign.shape, dtype=jnp.int32),
            vmem(2 * HALF, tokens, dtype=F32),
            vmem(*split_weight.shape),
            vmem(*mask_weight.shape),
            vmem(*qkv_weight.shape),
            vmem(*out_weight.shape),
            vmem(width, 2 * D),
            vmem(width, 2 * D),
            vmem(frames, width, dtype=F32),
            vmem(frames, width, dtype=F32),
            vmem(PAD, width),
            vmem(PAD, width),
            vmem(1, width, dtype=F32),
            vmem(tokens, width),
            vmem(frames, 128, dtype=F32),
            vmem(3, frames, 128, dtype=F32),
            vmem(2, 4, tokens, D),
            vmem(2, 2, tokens, D),
            vmem(2, tokens, D),
            vmem(2, tokens, D),
            vmem(HEADS, tokens, tokens, dtype=F32),
            vmem(3 * INNER, tokens),
            vmem(INNER, tokens),
            vmem(3 * INNER, tokens),
            vmem(INNER, 4 * D),
            vmem(4, tokens, D),
            vmem(tokens, 2 * D),
            vmem(half, 4 * D),
            vmem(2, half, columns),
            [
                vmem(max(x_size - 1, 1), half // x_size, columns),
                vmem(y_size - 1, half // y_size, columns),
            ],
            [vmem(half // x_size, columns), vmem(half // y_size, columns)],
            [vmem(y_size - 1, last, columns), vmem(max(x_size - 1, 1), last, columns)],
            vmem(8, 8, D, dtype=F32),
            vmem(7, 8, D, dtype=F32),
            vmem(8, 8, D, dtype=F32),
            [vmem(half // x_size, columns), vmem(half // y_size, columns)],
            pltpu.SemaphoreType.DMA((8,)),
            pltpu.SemaphoreType.DMA((copies,)),
            pltpu.SemaphoreType.DMA((copies,)),
        ],
        compiler_params=pltpu.CompilerParams(
            vmem_limit_bytes=VMEM_BYTES, collective_id=0, has_side_effects=True
        ),
    )(
        *(
            pltpu.with_memory_space_constraint(operand, pltpu.HBM)
            for operand in (
                spectrum,
                mask_cotangent,
                assign,
                jnp.asarray(rotary_table(tokens)),
                split_weight,
                mask_weight,
                qkv_weight,
                out_weight,
            )
        )
    )
    return tuple(
        pl.pallas_call(
            store_kernel,
            out_shape=[
                jax.ShapeDtypeStruct((frames, width), F32),
                jax.ShapeDtypeStruct(qkv_weight.shape, F32),
                jax.ShapeDtypeStruct(out_weight.shape, F32),
            ],
            in_specs=[inside] * 2,
            out_specs=[outside] * 3,
            scratch_shapes=[
                vmem(*qkv_weight.shape, dtype=F32),
                vmem(*out_weight.shape, dtype=F32),
                pltpu.SemaphoreType.DMA((5,)),
            ],
            compiler_params=pltpu.CompilerParams(vmem_limit_bytes=VMEM_BYTES // 4),
        )(gathered, rows)
    )


def solution(mesh):
    return jax.shard_map(
        functools.partial(on_device, axis_sizes(mesh.shape["tm"])),
        mesh=mesh,
        in_specs=(
            P("tm", "band"),
            P(),
            P("band", None, None, None),
            P(),
            P(),
            P("band", None, None, None),
            P("tm", "band"),
        ),
        out_specs=(P("tm", "band"), P(), P()),
        check_vma=False,
    )
```

```python
import functools
import math

import jax
import jax.numpy as jnp
import numpy as np
from jax import lax
from jax.experimental import pallas as pl
from jax.experimental.pallas import tpu as pltpu
from jax.sharding import PartitionSpec as P

HEADS = 8
HEAD_DIM = 64
HALF = 32
D = 384
INNER = 512
BANDS = 60
PAD = 64
FEATS = 8
EPSILON = 1e-05
VMEM_BYTES = 50 * 1024 * 1024
BF16 = jnp.bfloat16
F32 = jnp.float32

NN = (((1,), (0,)), ((), ()))
NT = (((1,), (1,)), ((), ()))
TN = (((0,), (0,)), ((), ()))


def dot(left, right, dims=NN):
    return lax.dot_general(left, right, dims, preferred_element_type=F32)


def split_three(values):
    high = values.astype(BF16)
    rest = values - high.astype(F32)
    middle = rest.astype(BF16)
    low = (rest - middle.astype(F32)).astype(BF16)
    return high, middle, low


def iota(shape, dim):
    return lax.broadcasted_iota(jnp.int32, shape, dim)


def segment_masks(assign_ref, first_bin, bin_count):
    rising = assign_ref[:, 0, pl.ds(first_bin, bin_count)].astype(F32).astype(BF16)
    falling = assign_ref[:, 1, pl.ds(first_bin, bin_count)].astype(F32).astype(BF16)
    row, column = iota((PAD, BANDS), 0), iota((PAD, BANDS), 1)
    same = jnp.where(row == column, 1.0, 0.0).astype(BF16)
    last = jnp.where((row == BANDS) & (column == BANDS - 1), 1.0, 0.0).astype(BF16)
    risen = dot(same, rising)
    segments = risen + dot(last, falling)
    bands = risen + dot(same, falling)
    width = bin_count * FEATS
    repeat = jnp.where(
        iota((bin_count, width), 1) // FEATS == iota((bin_count, width), 0), 1.0, 0.0
    ).astype(BF16)
    return dot(segments.astype(BF16), repeat), bands.astype(BF16), repeat


def pack_weight(weight_ref, packed_ref):
    bin_count = weight_ref.shape[0]
    step = 32
    for first in range(0, bin_count, step):
        for side in range(2):
            block = weight_ref[first : first + step, side].astype(F32)
            packed_ref[first * FEATS : (first + step) * FEATS, side * D : (side + 1) * D] = (
                block.reshape(step * FEATS, D).astype(BF16)
            )


def band_sums(rows_ref, first_row, mask_ref, packed_ref, masked_ref):
    tokens = masked_ref.shape[0]
    mask = mask_ref[...]
    for frame in range(tokens // PAD):
        row = rows_ref[pl.ds(first_row + frame, 1), :].astype(BF16)
        masked_ref[frame * PAD : (frame + 1) * PAD, :] = mask * row
    total = dot(masked_ref[...], packed_ref[...])
    shifted = pltpu.roll(total[:, D:], tokens - 1, 0)
    in_band = iota((tokens, 1), 0) % PAD < BANDS
    return jnp.where(in_band, total[:, :D] + shifted, 0.0).astype(BF16)


def whole_kernel(
    sizes,
    spectrum_hbm,
    cotangent_hbm,
    assign_hbm,
    table_hbm,
    split_hbm,
    mask_hbm,
    qkv_hbm,
    out_hbm,
    mask_out,
    gathered,
    spectrum_ref,
    cotangent_ref,
    assign_ref,
    table_ref,
    split_raw,
    mask_raw,
    qkv_ref,
    out_weight_ref,
    split_packed,
    mask_packed,
    spectrum_rows,
    cotangent_rows,
    segment_ref,
    scaled_ref,
    inverse_ref,
    masked_ref,
    energy_ref,
    energies,
    parts,
    from_core,
    to_chip,
    from_chip,
    probs_ref,
    heads_ref,
    attended_ref,
    grad_projected_ref,
    qkv_turned,
    out_turned,
    bias_ref,
    normed_ref,
    normed_in_other,
    attended_other,
    grad_hidden_ref,
    grad_hidden_other,
    grad_projected_other,
    normed_all,
    pair_ref,
    pair_sum,
    first_in,
    first_sum,
    second_in,
    second_sum,
    depth_in,
    depth_all,
    second_all,
    load,
    send,
    receive,
):
    x_size, y_high, z_size = sizes
    y_size = y_high * 2
    me_tm, me = lax.axis_index("tm"), lax.axis_index("band")
    chip, core = me // 2, me % 2
    x = me_tm // (y_high * z_size)
    y = (me_tm // z_size) % y_high * 2 + chip
    z = me_tm % z_size
    tokens = masked_ref.shape[0]
    frames = tokens // PAD

    def device(at_x, at_y, at_z, at_core):
        return ((at_x * y_high + at_y // 2) * z_size + at_z, (at_y % 2) * 2 + at_core)

    other_core = (me_tm, chip * 2 + 1 - core)
    other_chip = (me_tm, (1 - chip) * 2 + core)
    diagonal = (me_tm, (1 - chip) * 2 + 1 - core)
    x_peers = [device(lax.rem(x + s, x_size), y, z, core) for s in range(1, x_size)]
    y_peers = [device(x, lax.rem(y + s, y_size), z, core) for s in range(1, y_size)]
    z_peers = [device(x, y, lax.rem(z + s, z_size), core) for s in range(1, z_size)]
    everyone = [other_core, diagonal] + x_peers + y_peers + z_peers
    barrier = pltpu.get_barrier_semaphore()
    for peer in everyone:
        pl.semaphore_signal(barrier, inc=1, device_id=peer, device_id_type=pl.DeviceIdType.MESH)
    loads = []
    for index, (source, target) in enumerate(
        (
            (assign_hbm, assign_ref),
            (spectrum_hbm, spectrum_ref),
            (split_hbm, split_raw),
            (cotangent_hbm, cotangent_ref),
            (mask_hbm, mask_raw),
            (qkv_hbm, qkv_ref),
            (out_hbm, out_weight_ref),
            (table_hbm, table_ref),
        )
    ):
        copy = pltpu.make_async_copy(source, target, load.at[index])
        copy.start()
        loads.append(copy)
    def far_first(size):
        return sorted(range(1, size), key=lambda s: -min(s, size - s))

    next_index = [0]
    started = []

    def begin(source, target, to):
        index = next_index[0]
        next_index[0] += 1
        copy = pltpu.make_async_remote_copy(
            src_ref=source,
            dst_ref=target,
            send_sem=send.at[index],
            recv_sem=receive.at[index],
            device_id=to,
            device_id_type=pl.DeviceIdType.MESH,
        )
        copy.start()
        started.append(copy)
        return copy

    def drain():
        while started:
            started.pop(0).wait_send()

    bin_count = split_raw.shape[0]
    first_bin = pl.multiple_of(me * bin_count, bin_count)
    loads[0].wait()
    segment_mask, bands, repeat = segment_masks(assign_ref, first_bin, bin_count)
    segment_ref[...] = segment_mask.astype(BF16)
    loads[1].wait()
    spectrum = spectrum_ref[...].astype(F32)
    spectrum_rows[...] = spectrum

    quarters = [
        (1 - chip) * 2 + 1 - core,
        (1 - chip) * 2 + core,
        chip * 2 + 1 - core,
        me,
    ]
    energy_copies = []
    across = [None, None]
    seconds_in = [None, None]
    for item in range(2):
        loads[2 + 2 * item].wait()
        raw, packed = ((split_raw, split_packed), (mask_raw, mask_packed))[item]
        rows_ref, mask_ref = ((spectrum_rows, segment_ref), (cotangent_rows, scaled_ref))[item]
        pack_weight(raw, packed)
        for slot in range(4):
            parts[item, slot] = band_sums(
                rows_ref, quarters[slot] * frames, mask_ref, packed, masked_ref
            )
            if slot == 0:
                if item == 0:
                    pl.semaphore_wait(barrier, len(everyone))
                first = begin(parts.at[item, 0], from_core.at[item, 0], other_core)
                if item == 0:
                    band_mask = dot(bands, repeat)
                    inverse = 1.0 / jnp.sum(band_mask, axis=0, keepdims=True)
                    inverse_ref[...] = inverse
                    scaled_ref[...] = (segment_mask * inverse).astype(BF16)
                    loads[3].wait()
                    cotangent_rows[...] = cotangent_ref[...].astype(F32)
                    band_bf = band_mask.astype(BF16)
                    energy = jnp.zeros((spectrum.shape[0], PAD), F32)
                    for term in split_three(spectrum * spectrum):
                        energy += dot(term, band_bf, NT)
                    energy_ref[...] = jnp.zeros_like(energy_ref)
                    energy_ref[:, :PAD] = energy
                    for index, peer in enumerate((other_core, other_chip, diagonal)):
                        energy_copies.append(begin(energy_ref, energies.at[index], peer))
            if slot == 1:
                first.wait_recv()
                to_chip[item] = (
                    parts[item, 1].astype(F32) + from_core[item, 0].astype(F32)
                ).astype(BF16)
                across[item] = begin(to_chip.at[item], from_chip.at[item], other_chip)
            if slot == 2:
                seconds_in[item] = begin(parts.at[item, 2], from_core.at[item, 1], other_core)

    def reduced(item):
        seconds_in[item].wait_recv()
        across[item].wait_recv()
        own = parts[item, 3].astype(F32) + from_core[item, 1].astype(F32)
        return own + from_chip[item].astype(F32)

    for copy in energy_copies:
        copy.wait_recv()
    total_energy = energy_ref[...] + energies[0] + energies[1] + energies[2]
    both = (assign_ref[:, 0, :] + assign_ref[:, 1, :]).astype(F32).astype(BF16)
    bins = both.shape[1]
    band_sizes = FEATS * dot(jnp.ones((8, bins), BF16), both, NT)[:1]
    ratio = total_energy[:, :BANDS] / jnp.maximum(band_sizes, 1.0)
    lane = iota((BANDS, tokens), 1)
    spread = jnp.where(lane % PAD == iota((BANDS, tokens), 0), 1.0, 0.0).astype(BF16)
    rows = total_energy.shape[0]
    energy = jnp.zeros((rows, tokens), F32)
    for term in split_three(ratio):
        energy += dot(term, spread)
    mine = iota((rows, tokens), 0) == me * frames + iota((rows, tokens), 1) // PAD
    energy = jnp.sum(jnp.where(mine, energy, 0.0), axis=0, keepdims=True)
    in_band = iota((1, tokens), 1) % PAD < BANDS
    for copy in loads[5:]:
        copy.wait()
    qkv_turned[...] = jnp.transpose(qkv_ref[...])
    out_turned[...] = jnp.transpose(out_weight_ref[...])
    key_lane, query_lane = iota((tokens, tokens), 0), iota((tokens, tokens), 1)
    allowed = (key_lane // PAD == query_lane // PAD) & (key_lane % PAD < BANDS)
    bias_ref[...] = jnp.where(allowed, 0.0, -1e30)

    hidden_in = (jnp.transpose(reduced(0)) * lax.rsqrt(energy + EPSILON)).astype(BF16)
    hidden_in = hidden_in.astype(F32)
    normed_in = (
        hidden_in
        * lax.rsqrt(jnp.mean(hidden_in * hidden_in, axis=0, keepdims=True) + EPSILON)
    ).astype(BF16)
    normed_ref[...] = normed_in
    swaps = [begin(normed_ref, normed_in_other, other_core)]
    projected = dot(qkv_turned[...], normed_in)
    cos, sin = table_ref[:HALF, :], table_ref[HALF:, :]
    scale = HEAD_DIM**-0.5
    for head in range(HEADS):
        for part in range(2):
            base = part * INNER + head * HEAD_DIM
            front = projected[base : base + HALF]
            back = projected[base + HALF : base + HEAD_DIM]
            factor = scale if part == 0 else 1.0
            heads_ref[base : base + HALF, :] = ((front * cos - back * sin) * factor).astype(BF16)
            heads_ref[base + HALF : base + HEAD_DIM, :] = (
                (front * sin + back * cos) * factor
            ).astype(BF16)
    heads_ref[2 * INNER :, :] = projected[2 * INNER :].astype(BF16)

    def part_of(part, head):
        base = part * INNER + head * HEAD_DIM
        return heads_ref[base : base + HEAD_DIM, :]

    for head in range(HEADS):
        scores = dot(part_of(1, head), part_of(0, head), TN) + bias_ref[...]
        powers = jnp.exp(scores - jnp.max(scores, axis=0, keepdims=True))
        probs = powers / jnp.sum(powers, axis=0, keepdims=True)
        probs_ref[head] = probs
        attended_ref[head * HEAD_DIM : (head + 1) * HEAD_DIM, :] = dot(
            part_of(2, head), probs.astype(BF16)
        ).astype(BF16)
    inner_half = INNER // 2
    own_inner = pl.ds(pl.multiple_of(core * inner_half, inner_half), inner_half)
    other_inner = pl.ds(pl.multiple_of((1 - core) * inner_half, inner_half), inner_half)
    swaps.append(begin(attended_ref.at[other_inner, :], attended_other, other_core))
    mixed = dot(out_turned[...], attended_ref[...])
    hidden_out = (hidden_in + mixed).astype(BF16).astype(F32)
    inverse = lax.rsqrt(jnp.mean(hidden_out * hidden_out, axis=0, keepdims=True) + EPSILON)
    normed_out = jnp.where(in_band, hidden_out * inverse, 0.0)
    normed_all[me] = jnp.transpose(normed_out).astype(BF16)
    to_chip_rows = begin(normed_all.at[me], normed_all.at[me], other_chip)
    to_core_rows = begin(normed_all.at[me], normed_all.at[me], other_core)

    upstream = jnp.transpose(reduced(1))
    inner = jnp.mean(upstream * hidden_out, axis=0, keepdims=True)
    grad_hidden = (
        inverse * upstream - hidden_out * (inverse * inverse * inverse) * inner
    ).astype(BF16)
    grad_attended = dot(out_weight_ref[...], grad_hidden).astype(BF16)
    grad_hidden_ref[...] = grad_hidden
    swaps.append(begin(grad_hidden_ref, grad_hidden_other, other_core))
    for head in range(HEADS):
        probs = probs_ref[head]
        grad_head = grad_attended[head * HEAD_DIM : (head + 1) * HEAD_DIM]
        grad_probs = dot(part_of(2, head), grad_head, TN)
        row_sum = jnp.sum(grad_probs * probs, axis=0, keepdims=True)
        grad_scores = (probs * (grad_probs - row_sum)).astype(BF16)
        grad_values = dot(grad_head, probs.astype(BF16), NT)
        grad_queries = dot(part_of(1, head), grad_scores) * scale
        grad_keys = dot(part_of(0, head), grad_scores, NT)
        for part, grad in ((0, grad_queries), (1, grad_keys)):
            base = part * INNER + head * HEAD_DIM
            front, back = grad[:HALF], grad[HALF:]
            grad_projected_ref[base : base + HALF, :] = (front * cos + back * sin).astype(BF16)
            grad_projected_ref[base + HALF : base + HEAD_DIM, :] = (
                back * cos - front * sin
            ).astype(BF16)
        base = 2 * INNER + head * HEAD_DIM
        grad_projected_ref[base : base + HEAD_DIM, :] = grad_values.astype(BF16)
    columns = 3 * INNER // 2
    own_columns = pl.ds(pl.multiple_of(core * columns, columns), columns)
    other_columns = pl.ds(pl.multiple_of((1 - core) * columns, columns), columns)
    last_swap = begin(
        grad_projected_ref.at[other_columns, :], grad_projected_other, other_core
    )

    def mask_rows(quarter):
        normed = normed_all[quarter]
        pair_ref[:, :D] = normed
        pair_ref[:, D:] = pltpu.roll(normed.astype(F32), 1, 0).astype(BF16)
        estimate = dot(pair_ref[...], mask_packed[...], NT)
        mask = segment_ref[...].astype(F32)
        for frame in range(frames):
            block = estimate[frame * PAD : (frame + 1) * PAD]
            mask_out[pl.ds(quarter * frames + frame, 1), :] = (
                jnp.sum(block * mask, axis=0, keepdims=True) * inverse_ref[...]
            )

    half = INNER // 2
    quarter = INNER // 4
    for copy in swaps:
        copy.wait_recv()
    out_grad = dot(attended_ref[own_inner, :], grad_hidden, NT) + dot(
        attended_other[...], grad_hidden_other[...], NT
    )
    for block in range(2):
        pair_sum[1, quarter:, block * D : (block + 1) * D] = out_grad[
            block * quarter : (block + 1) * quarter
        ].astype(BF16)
    own_grad = dot(normed_in, grad_projected_ref[own_columns, :], NT)
    mask_rows(me)
    last_swap.wait_recv()
    own_grad = (own_grad + dot(normed_in_other[...], grad_projected_other[...], NT)).astype(BF16)
    pair_sum[0] = own_grad[:half]
    pair_sum[1, :quarter, :] = own_grad[half:]

    axes = ((x, x_size, x_peers), (y, y_size, y_peers))
    counts = [half // x_size, half // y_size]
    firsts = ({}, {})
    for step in far_first(4):
        for part in range(2):
            at, size, peers = axes[part]
            if step < size:
                count = counts[part]
                there = pl.ds(pl.multiple_of(lax.rem(at + step, size) * count, count), count)
                firsts[part][step] = begin(
                    pair_sum.at[part, there, :], first_in[part].at[step - 1], peers[step - 1]
                )
    to_core_rows.wait_recv()
    mask_rows(chip * 2 + 1 - core)
    to_chip_rows.wait_recv()
    chip_rows = normed_all.at[(1 - chip) * 2 + core]
    onward = begin(chip_rows, chip_rows, other_core)
    for part in range(2):
        at, size, peers = axes[part]
        count = counts[part]
        here = pl.ds(pl.multiple_of(at * count, count), count)
        total = pair_sum[part, here, :].astype(F32)
        for step in range(1, size):
            firsts[part][step].wait_recv()
            total += first_in[part][step - 1].astype(F32)
        first_sum[part][...] = total.astype(BF16)

    last_rows = half // (x_size * y_size)
    seconds = ({}, {})
    for part in range(2):
        at, size, peers = axes[1 - part]
        for step in far_first(size):
            there = pl.ds(
                pl.multiple_of(lax.rem(at + step, size) * last_rows, last_rows), last_rows
            )
            seconds[part][step] = begin(
                first_sum[part].at[there, :], second_in[part].at[step - 1], peers[step - 1]
            )
    mask_rows((1 - chip) * 2 + core)
    chunk_rows, chunk_columns = 8, columns // 2
    for part in range(2):
        at, size, peers = axes[1 - part]
        here = pl.ds(pl.multiple_of(at * last_rows, last_rows), last_rows)
        total = first_sum[part][here, :].astype(F32)
        for step in range(1, size):
            seconds[part][step].wait_recv()
            total += second_in[part][step - 1].astype(F32)
        if z_size == 1:
            second_all[part][here, :] = total.astype(BF16)
        else:
            for block in range(4):
                r, c = block // 2 * chunk_rows, block % 2 * chunk_columns
                second_sum[part * 4 + block] = total[r : r + chunk_rows, c : c + chunk_columns]

    if z_size > 1:
        depths = {
            s: begin(second_sum.at[lax.rem(z + s, z_size)], depth_in.at[s - 1], z_peers[s - 1])
            for s in far_first(z_size)
        }
    onward.wait_recv()
    mask_rows((1 - chip) * 2 + 1 - core)
    drain()
    if z_size > 1:
        total = second_sum[z]
        for step in range(1, z_size):
            depths[step].wait_recv()
            total += depth_in[step - 1]
        depth_all[z] = total
        backs = [
            begin(depth_all.at[z], depth_all.at[z], z_peers[s - 1]) for s in far_first(z_size)
        ]
        for copy in backs:
            copy.wait_recv()
        for part in range(2):
            at = axes[1 - part][0]
            here = pl.ds(pl.multiple_of(at * last_rows, last_rows), last_rows)
            rows_of = []
            for high in range(2):
                rows_of.append(
                    jnp.concatenate(
                        [depth_all[part * 4 + high * 2], depth_all[part * 4 + high * 2 + 1]], axis=1
                    )
                )
            second_all[part][here, :] = jnp.concatenate(rows_of, axis=0).astype(BF16)

    backs = ([], [])
    for part in range(2):
        at, size, peers = axes[1 - part]
        here = pl.ds(pl.multiple_of(at * last_rows, last_rows), last_rows)
        for step in far_first(size):
            block = second_all[part].at[here, :]
            backs[part].append(begin(block, block, peers[step - 1]))
    spread = ([], [])
    for part in range(2):
        for copy in backs[part]:
            copy.wait_recv()
        at, size, peers = axes[part]
        count = counts[part]
        here = pl.ds(pl.multiple_of(at * count, count), count)
        target = gathered.at[part, core, here, :]
        for step in far_first(size):
            spread[part].append(begin(second_all[part], target, peers[step - 1]))
        gathered[part, core, here, :] = second_all[part][...]
    mirrored = []
    for part in range(2):
        for copy in spread[part]:
            copy.wait_recv()
        whole = gathered.at[part, core]
        mirrored.append(begin(whole, whole, other_core))
    drain()
    for copy in mirrored:
        copy.wait_recv()


def store_kernel(gathered_ref, rows_ref, mask_hbm, qkv_hbm, out_hbm, qkv_ref, out_ref, store):
    copies = [pltpu.make_async_copy(rows_ref, mask_hbm, store.at[0])]
    copies[0].start()
    columns = gathered_ref.shape[3]
    quarter = INNER // 4
    for block in range(3):
        here = slice(block * quarter, (block + 1) * quarter)
        there = slice(block % 2 * quarter, (block % 2 + 1) * quarter)
        for core in range(2):
            qkv_ref[here, core * columns : (core + 1) * columns] = gathered_ref[
                block // 2, core, there, :
            ].astype(F32)
        copies.append(
            pltpu.make_async_copy(qkv_ref.at[here, :], qkv_hbm.at[here, :], store.at[1 + block])
        )
        copies[-1].start()
    for block in range(4):
        out_ref[block * quarter : (block + 1) * quarter, :] = gathered_ref[
            1, block // 2, quarter:, block % 2 * D : (block % 2 + 1) * D
        ].astype(F32)
    copies.append(pltpu.make_async_copy(out_ref, out_hbm, store.at[4]))
    copies[-1].start()
    for copy in copies:
        copy.wait()


def rotary_table(tokens):
    position = (np.arange(tokens) % PAD).astype(np.float64)[None, :]
    frequency = np.exp(-math.log(10000.0) * np.arange(HALF) / HALF)[:, None]
    angles = position * frequency
    return np.concatenate([np.cos(angles), np.sin(angles)], axis=0).astype(np.float32)


def axis_sizes(tm_size):
    return {64: (4, 2, 8), 8: (4, 2, 1), 4: (4, 1, 1), 2: (2, 1, 1), 1: (1, 1, 1)}[tm_size]


def on_device(
    sizes, spectrum, band_assign, split_weight, qkv_weight, out_weight, mask_weight, mask_cotangent
):
    frames, width = spectrum.shape
    tokens = frames // 4 * PAD
    x_size, y_high, z_size = sizes
    y_size = 2 * y_high
    half, columns = INNER // 2, 2 * D
    last = half // (x_size * y_size)
    copies = 72

    def vmem(*shape, dtype=BF16):
        return pltpu.VMEM(shape, dtype)

    inside = pl.BlockSpec(memory_space=pltpu.VMEM)
    outside = pl.BlockSpec(memory_space=pltpu.HBM)
    assign = jnp.transpose(band_assign, (2, 0, 1))
    rows, gathered = pl.pallas_call(
        functools.partial(whole_kernel, sizes),
        out_shape=[
            jax.ShapeDtypeStruct((frames, width), F32),
            jax.ShapeDtypeStruct((2, 2, half, columns), BF16),
        ],
        in_specs=[outside] * 8,
        out_specs=[inside] * 2,
        scratch_shapes=[
            vmem(frames, width),
            vmem(frames, width),
            vmem(*assign.shape, dtype=jnp.int32),
            vmem(2 * HALF, tokens, dtype=F32),
            vmem(*split_weight.shape),
            vmem(*mask_weight.shape),
            vmem(*qkv_weight.shape),
            vmem(*out_weight.shape),
            vmem(width, 2 * D),
            vmem(width, 2 * D),
            vmem(frames, width, dtype=F32),
            vmem(frames, width, dtype=F32),
            vmem(PAD, width),
            vmem(PAD, width),
            vmem(1, width, dtype=F32),
            vmem(tokens, width),
            vmem(frames, 128, dtype=F32),
            vmem(3, frames, 128, dtype=F32),
            vmem(2, 4, tokens, D),
            vmem(2, 2, tokens, D),
            vmem(2, tokens, D),
            vmem(2, tokens, D),
            vmem(HEADS, tokens, tokens, dtype=F32),
            vmem(3 * INNER, tokens),
            vmem(INNER, tokens),
            vmem(3 * INNER, tokens),
            vmem(3 * INNER, D),
            vmem(D, INNER),
            vmem(tokens, tokens, dtype=F32),
            vmem(D, tokens),
            vmem(D, tokens),
            vmem(INNER // 2, tokens),
            vmem(D, tokens),
            vmem(D, tokens),
            vmem(3 * INNER // 2, tokens),
            vmem(4, tokens, D),
            vmem(tokens, 2 * D),
            vmem(2, half, columns),
            [
                vmem(max(x_size - 1, 1), half // x_size, columns),
                vmem(y_size - 1, half // y_size, columns),
            ],
            [vmem(half // x_size, columns), vmem(half // y_size, columns)],
            [vmem(y_size - 1, last, columns), vmem(max(x_size - 1, 1), last, columns)],
            vmem(8, 8, D, dtype=F32),
            vmem(7, 8, D, dtype=F32),
            vmem(8, 8, D, dtype=F32),
            [vmem(half // x_size, columns), vmem(half // y_size, columns)],
            pltpu.SemaphoreType.DMA((8,)),
            pltpu.SemaphoreType.DMA((copies,)),
            pltpu.SemaphoreType.DMA((copies,)),
        ],
        compiler_params=pltpu.CompilerParams(
            vmem_limit_bytes=VMEM_BYTES, collective_id=0, has_side_effects=True
        ),
    )(
        *(
            pltpu.with_memory_space_constraint(operand, pltpu.HBM)
            for operand in (
                spectrum,
                mask_cotangent,
                assign,
                jnp.asarray(rotary_table(tokens)),
                split_weight,
                mask_weight,
                qkv_weight,
                out_weight,
            )
        )
    )
    return tuple(
        pl.pallas_call(
            store_kernel,
            out_shape=[
                jax.ShapeDtypeStruct((frames, width), F32),
                jax.ShapeDtypeStruct(qkv_weight.shape, F32),
                jax.ShapeDtypeStruct(out_weight.shape, F32),
            ],
            in_specs=[inside] * 2,
            out_specs=[outside] * 3,
            scratch_shapes=[
                vmem(*qkv_weight.shape, dtype=F32),
                vmem(*out_weight.shape, dtype=F32),
                pltpu.SemaphoreType.DMA((5,)),
            ],
            compiler_params=pltpu.CompilerParams(vmem_limit_bytes=VMEM_BYTES // 4),
        )(gathered, rows)
    )


def solution(mesh):
    return jax.shard_map(
        functools.partial(on_device, axis_sizes(mesh.shape["tm"])),
        mesh=mesh,
        in_specs=(
            P("tm", "band"),
            P(),
            P("band", None, None, None),
            P(),
            P(),
            P("band", None, None, None),
            P("tm", "band"),
        ),
        out_specs=(P("tm", "band"), P(), P()),
        check_vma=False,
    )
```

```python
import functools
import math

import jax
import jax.numpy as jnp
import numpy as np
from jax import lax
from jax.experimental import pallas as pl
from jax.experimental.pallas import tpu as pltpu
from jax.sharding import PartitionSpec as P

HEADS = 8
HEAD_DIM = 64
HALF = 32
D = 384
INNER = 512
BANDS = 60
PAD = 64
FEATS = 8
EPSILON = 1e-05
VMEM_BYTES = 50 * 1024 * 1024
BF16 = jnp.bfloat16
F32 = jnp.float32

NN = (((1,), (0,)), ((), ()))
NT = (((1,), (1,)), ((), ()))
TN = (((0,), (0,)), ((), ()))


def dot(left, right, dims=NN):
    return lax.dot_general(left, right, dims, preferred_element_type=F32)


def split_three(values):
    high = values.astype(BF16)
    rest = values - high.astype(F32)
    middle = rest.astype(BF16)
    low = (rest - middle.astype(F32)).astype(BF16)
    return high, middle, low


def iota(shape, dim):
    return lax.broadcasted_iota(jnp.int32, shape, dim)


def segment_masks(assign_ref, first_bin, bin_count):
    rising = assign_ref[:, 0, pl.ds(first_bin, bin_count)].astype(F32).astype(BF16)
    falling = assign_ref[:, 1, pl.ds(first_bin, bin_count)].astype(F32).astype(BF16)
    row, column = iota((PAD, BANDS), 0), iota((PAD, BANDS), 1)
    same = jnp.where(row == column, 1.0, 0.0).astype(BF16)
    last = jnp.where((row == BANDS) & (column == BANDS - 1), 1.0, 0.0).astype(BF16)
    risen = dot(same, rising)
    segments = risen + dot(last, falling)
    bands = risen + dot(same, falling)
    width = bin_count * FEATS
    repeat = jnp.where(
        iota((bin_count, width), 1) // FEATS == iota((bin_count, width), 0), 1.0, 0.0
    ).astype(BF16)
    return dot(segments.astype(BF16), repeat), bands.astype(BF16), repeat


def pack_weight(weight_ref, packed_ref):
    bin_count = weight_ref.shape[0]
    step = 32
    for first in range(0, bin_count, step):
        for side in range(2):
            block = weight_ref[first : first + step, side].astype(F32)
            packed_ref[first * FEATS : (first + step) * FEATS, side * D : (side + 1) * D] = (
                block.reshape(step * FEATS, D).astype(BF16)
            )


def band_sums(rows_ref, first_row, mask_ref, packed_ref, masked_ref):
    tokens = masked_ref.shape[0]
    mask = mask_ref[...]
    for frame in range(tokens // PAD):
        row = rows_ref[pl.ds(first_row + frame, 1), :].astype(BF16)
        masked_ref[frame * PAD : (frame + 1) * PAD, :] = mask * row
    total = dot(masked_ref[...], packed_ref[...])
    shifted = pltpu.roll(total[:, D:], tokens - 1, 0)
    in_band = iota((tokens, 1), 0) % PAD < BANDS
    return jnp.where(in_band, total[:, :D] + shifted, 0.0).astype(BF16)


def whole_kernel(
    sizes,
    spectrum_hbm,
    cotangent_hbm,
    assign_hbm,
    table_hbm,
    split_hbm,
    mask_hbm,
    qkv_hbm,
    out_hbm,
    mask_out,
    gathered,
    spectrum_ref,
    cotangent_ref,
    assign_ref,
    table_ref,
    split_raw,
    mask_raw,
    qkv_ref,
    out_weight_ref,
    split_packed,
    mask_packed,
    spectrum_rows,
    cotangent_rows,
    segment_ref,
    scaled_ref,
    inverse_ref,
    masked_ref,
    energy_ref,
    energies,
    parts,
    from_core,
    to_chip,
    from_chip,
    probs_ref,
    heads_ref,
    attended_ref,
    grad_projected_ref,
    qkv_turned,
    out_turned,
    bias_ref,
    normed_ref,
    normed_in_other,
    attended_other,
    grad_hidden_ref,
    grad_hidden_other,
    grad_projected_other,
    normed_all,
    pair_ref,
    pair_sum,
    first_in,
    first_sum,
    second_in,
    second_sum,
    depth_in,
    depth_all,
    second_all,
    load,
    send,
    receive,
):
    x_size, y_high, z_size = sizes
    y_size = y_high * 2
    me_tm, me = lax.axis_index("tm"), lax.axis_index("band")
    chip, core = me // 2, me % 2
    x = me_tm // (y_high * z_size)
    y = (me_tm // z_size) % y_high * 2 + chip
    z = me_tm % z_size
    tokens = masked_ref.shape[0]
    frames = tokens // PAD

    def device(at_x, at_y, at_z, at_core):
        return ((at_x * y_high + at_y // 2) * z_size + at_z, (at_y % 2) * 2 + at_core)

    other_core = (me_tm, chip * 2 + 1 - core)
    other_chip = (me_tm, (1 - chip) * 2 + core)
    diagonal = (me_tm, (1 - chip) * 2 + 1 - core)
    x_peers = [device(lax.rem(x + s, x_size), y, z, core) for s in range(1, x_size)]
    y_peers = [device(x, lax.rem(y + s, y_size), z, core) for s in range(1, y_size)]
    z_peers = [device(x, y, lax.rem(z + s, z_size), core) for s in range(1, z_size)]
    everyone = [other_core, diagonal] + x_peers + y_peers + z_peers
    barrier = pltpu.get_barrier_semaphore()
    for peer in everyone:
        pl.semaphore_signal(barrier, inc=1, device_id=peer, device_id_type=pl.DeviceIdType.MESH)
    loads = []
    for index, (source, target) in enumerate(
        (
            (assign_hbm, assign_ref),
            (spectrum_hbm, spectrum_ref),
            (split_hbm, split_raw),
            (cotangent_hbm, cotangent_ref),
            (mask_hbm, mask_raw),
            (qkv_hbm, qkv_ref),
            (out_hbm, out_weight_ref),
            (table_hbm, table_ref),
        )
    ):
        copy = pltpu.make_async_copy(source, target, load.at[index])
        copy.start()
        loads.append(copy)
    def far_first(size):
        return sorted(range(1, size), key=lambda s: -min(s, size - s))

    next_index = [0]
    started = []

    def begin(source, target, to):
        index = next_index[0]
        next_index[0] += 1
        copy = pltpu.make_async_remote_copy(
            src_ref=source,
            dst_ref=target,
            send_sem=send.at[index],
            recv_sem=receive.at[index],
            device_id=to,
            device_id_type=pl.DeviceIdType.MESH,
        )
        copy.start()
        started.append(copy)
        return copy

    def drain():
        while started:
            started.pop(0).wait_send()

    bin_count = split_raw.shape[0]
    first_bin = pl.multiple_of(me * bin_count, bin_count)
    loads[0].wait()
    segment_mask, bands, repeat = segment_masks(assign_ref, first_bin, bin_count)
    segment_ref[...] = segment_mask.astype(BF16)
    loads[1].wait()
    spectrum = spectrum_ref[...].astype(F32)
    spectrum_rows[...] = spectrum

    quarters = [
        (1 - chip) * 2 + 1 - core,
        (1 - chip) * 2 + core,
        chip * 2 + 1 - core,
        me,
    ]
    energy_copies = []
    across = [None, None]
    seconds_in = [None, None]
    for item in range(2):
        loads[2 + 2 * item].wait()
        raw, packed = ((split_raw, split_packed), (mask_raw, mask_packed))[item]
        rows_ref, mask_ref = ((spectrum_rows, segment_ref), (cotangent_rows, scaled_ref))[item]
        pack_weight(raw, packed)
        for slot in range(4):
            parts[item, slot] = band_sums(
                rows_ref, quarters[slot] * frames, mask_ref, packed, masked_ref
            )
            if slot == 0:
                if item == 0:
                    pl.semaphore_wait(barrier, len(everyone))
                first = begin(parts.at[item, 0], from_core.at[item, 0], other_core)
                if item == 0:
                    band_mask = dot(bands, repeat)
                    inverse = 1.0 / jnp.sum(band_mask, axis=0, keepdims=True)
                    inverse_ref[...] = inverse
                    scaled_ref[...] = (segment_mask * inverse).astype(BF16)
                    loads[3].wait()
                    cotangent_rows[...] = cotangent_ref[...].astype(F32)
                    band_bf = band_mask.astype(BF16)
                    energy = jnp.zeros((spectrum.shape[0], PAD), F32)
                    for term in split_three(spectrum * spectrum):
                        energy += dot(term, band_bf, NT)
                    energy_ref[...] = jnp.zeros_like(energy_ref)
                    energy_ref[:, :PAD] = energy
                    for index, peer in enumerate((other_core, other_chip, diagonal)):
                        energy_copies.append(begin(energy_ref, energies.at[index], peer))
            if slot == 1:
                first.wait_recv()
                to_chip[item] = (
                    parts[item, 1].astype(F32) + from_core[item, 0].astype(F32)
                ).astype(BF16)
                across[item] = begin(to_chip.at[item], from_chip.at[item], other_chip)
            if slot == 2:
                seconds_in[item] = begin(parts.at[item, 2], from_core.at[item, 1], other_core)

    def reduced(item):
        seconds_in[item].wait_recv()
        across[item].wait_recv()
        own = parts[item, 3].astype(F32) + from_core[item, 1].astype(F32)
        return own + from_chip[item].astype(F32)

    for copy in energy_copies:
        copy.wait_recv()
    total_energy = energy_ref[...] + energies[0] + energies[1] + energies[2]
    both = (assign_ref[:, 0, :] + assign_ref[:, 1, :]).astype(F32).astype(BF16)
    bins = both.shape[1]
    band_sizes = FEATS * dot(jnp.ones((8, bins), BF16), both, NT)[:1]
    ratio = total_energy[:, :BANDS] / jnp.maximum(band_sizes, 1.0)
    lane = iota((BANDS, tokens), 1)
    spread = jnp.where(lane % PAD == iota((BANDS, tokens), 0), 1.0, 0.0).astype(BF16)
    rows = total_energy.shape[0]
    energy = jnp.zeros((rows, tokens), F32)
    for term in split_three(ratio):
        energy += dot(term, spread)
    mine = iota((rows, tokens), 0) == me * frames + iota((rows, tokens), 1) // PAD
    energy = jnp.sum(jnp.where(mine, energy, 0.0), axis=0, keepdims=True)
    in_band = iota((1, tokens), 1) % PAD < BANDS
    for copy in loads[5:]:
        copy.wait()
    qkv_turned[...] = jnp.transpose(qkv_ref[...])
    out_turned[...] = jnp.transpose(out_weight_ref[...])
    key_lane, query_lane = iota((tokens, tokens), 0), iota((tokens, tokens), 1)
    allowed = (key_lane // PAD == query_lane // PAD) & (key_lane % PAD < BANDS)
    bias_ref[...] = jnp.where(allowed, 0.0, -1e30)

    hidden_in = (jnp.transpose(reduced(0)) * lax.rsqrt(energy + EPSILON)).astype(BF16)
    hidden_in = hidden_in.astype(F32)
    normed_in = (
        hidden_in
        * lax.rsqrt(jnp.mean(hidden_in * hidden_in, axis=0, keepdims=True) + EPSILON)
    ).astype(BF16)
    normed_ref[...] = normed_in
    swaps = [begin(normed_ref, normed_in_other, other_core)]
    projected = dot(qkv_turned[...], normed_in)
    cos, sin = table_ref[:HALF, :], table_ref[HALF:, :]
    scale = HEAD_DIM**-0.5
    for head in range(HEADS):
        for part in range(2):
            base = part * INNER + head * HEAD_DIM
            front = projected[base : base + HALF]
            back = projected[base + HALF : base + HEAD_DIM]
            factor = scale if part == 0 else 1.0
            heads_ref[base : base + HALF, :] = ((front * cos - back * sin) * factor).astype(BF16)
            heads_ref[base + HALF : base + HEAD_DIM, :] = (
                (front * sin + back * cos) * factor
            ).astype(BF16)
    heads_ref[2 * INNER :, :] = projected[2 * INNER :].astype(BF16)

    def part_of(part, head):
        base = part * INNER + head * HEAD_DIM
        return heads_ref[base : base + HEAD_DIM, :]

    for head in range(HEADS):
        scores = dot(part_of(1, head), part_of(0, head), TN) + bias_ref[...]
        powers = jnp.exp(scores - jnp.max(scores, axis=0, keepdims=True))
        probs = powers * (1.0 / jnp.sum(powers, axis=0, keepdims=True))
        probs_ref[head] = probs
        attended_ref[head * HEAD_DIM : (head + 1) * HEAD_DIM, :] = dot(
            part_of(2, head), probs.astype(BF16)
        ).astype(BF16)
    inner_half = INNER // 2
    own_inner = pl.ds(pl.multiple_of(core * inner_half, inner_half), inner_half)
    other_inner = pl.ds(pl.multiple_of((1 - core) * inner_half, inner_half), inner_half)
    swaps.append(begin(attended_ref.at[other_inner, :], attended_other, other_core))
    mixed = dot(out_turned[...], attended_ref[...])
    hidden_out = (hidden_in + mixed).astype(BF16).astype(F32)
    inverse = lax.rsqrt(jnp.mean(hidden_out * hidden_out, axis=0, keepdims=True) + EPSILON)
    normed_out = jnp.where(in_band, hidden_out * inverse, 0.0)
    normed_all[me] = jnp.transpose(normed_out).astype(BF16)
    to_chip_rows = begin(normed_all.at[me], normed_all.at[me], other_chip)
    to_core_rows = begin(normed_all.at[me], normed_all.at[me], other_core)

    upstream = jnp.transpose(reduced(1))
    inner = jnp.mean(upstream * hidden_out, axis=0, keepdims=True)
    grad_hidden = (
        inverse * upstream - hidden_out * (inverse * inverse * inverse) * inner
    ).astype(BF16)
    grad_attended = dot(out_weight_ref[...], grad_hidden).astype(BF16)
    grad_hidden_ref[...] = grad_hidden
    swaps.append(begin(grad_hidden_ref, grad_hidden_other, other_core))
    for head in range(HEADS):
        probs = probs_ref[head]
        grad_head = grad_attended[head * HEAD_DIM : (head + 1) * HEAD_DIM]
        grad_probs = dot(part_of(2, head), grad_head, TN)
        row_sum = jnp.sum(grad_probs * probs, axis=0, keepdims=True)
        grad_scores = (probs * (grad_probs - row_sum)).astype(BF16)
        grad_values = dot(grad_head, probs.astype(BF16), NT)
        grad_queries = dot(part_of(1, head), grad_scores) * scale
        grad_keys = dot(part_of(0, head), grad_scores, NT)
        for part, grad in ((0, grad_queries), (1, grad_keys)):
            base = part * INNER + head * HEAD_DIM
            front, back = grad[:HALF], grad[HALF:]
            grad_projected_ref[base : base + HALF, :] = (front * cos + back * sin).astype(BF16)
            grad_projected_ref[base + HALF : base + HEAD_DIM, :] = (
                back * cos - front * sin
            ).astype(BF16)
        base = 2 * INNER + head * HEAD_DIM
        grad_projected_ref[base : base + HEAD_DIM, :] = grad_values.astype(BF16)
    columns = 3 * INNER // 2
    own_columns = pl.ds(pl.multiple_of(core * columns, columns), columns)
    other_columns = pl.ds(pl.multiple_of((1 - core) * columns, columns), columns)
    last_swap = begin(
        grad_projected_ref.at[other_columns, :], grad_projected_other, other_core
    )

    def mask_rows(quarter):
        normed = normed_all[quarter]
        pair_ref[:, :D] = normed
        pair_ref[:, D:] = pltpu.roll(normed.astype(F32), 1, 0).astype(BF16)
        estimate = dot(pair_ref[...], mask_packed[...], NT)
        mask = segment_ref[...].astype(F32)
        for frame in range(frames):
            block = estimate[frame * PAD : (frame + 1) * PAD]
            mask_out[pl.ds(quarter * frames + frame, 1), :] = (
                jnp.sum(block * mask, axis=0, keepdims=True) * inverse_ref[...]
            )

    half = INNER // 2
    quarter = INNER // 4
    for copy in swaps:
        copy.wait_recv()
    out_grad = dot(attended_ref[own_inner, :], grad_hidden, NT) + dot(
        attended_other[...], grad_hidden_other[...], NT
    )
    for block in range(2):
        pair_sum[1, quarter:, block * D : (block + 1) * D] = out_grad[
            block * quarter : (block + 1) * quarter
        ].astype(BF16)
    own_grad = dot(normed_in, grad_projected_ref[own_columns, :], NT)
    mask_rows(me)
    last_swap.wait_recv()
    own_grad = (own_grad + dot(normed_in_other[...], grad_projected_other[...], NT)).astype(BF16)
    pair_sum[0] = own_grad[:half]
    pair_sum[1, :quarter, :] = own_grad[half:]

    axes = ((x, x_size, x_peers), (y, y_size, y_peers))
    counts = [half // x_size, half // y_size]
    firsts = ({}, {})
    for step in far_first(4):
        for part in range(2):
            at, size, peers = axes[part]
            if step < size:
                count = counts[part]
                there = pl.ds(pl.multiple_of(lax.rem(at + step, size) * count, count), count)
                firsts[part][step] = begin(
                    pair_sum.at[part, there, :], first_in[part].at[step - 1], peers[step - 1]
                )
    to_core_rows.wait_recv()
    mask_rows(chip * 2 + 1 - core)
    to_chip_rows.wait_recv()
    chip_rows = normed_all.at[(1 - chip) * 2 + core]
    onward = begin(chip_rows, chip_rows, other_core)
    for part in range(2):
        at, size, peers = axes[part]
        count = counts[part]
        here = pl.ds(pl.multiple_of(at * count, count), count)
        total = pair_sum[part, here, :].astype(F32)
        for step in range(1, size):
            firsts[part][step].wait_recv()
            total += first_in[part][step - 1].astype(F32)
        first_sum[part][...] = total.astype(BF16)

    last_rows = half // (x_size * y_size)
    seconds = ({}, {})
    for part in range(2):
        at, size, peers = axes[1 - part]
        for step in far_first(size):
            there = pl.ds(
                pl.multiple_of(lax.rem(at + step, size) * last_rows, last_rows), last_rows
            )
            seconds[part][step] = begin(
                first_sum[part].at[there, :], second_in[part].at[step - 1], peers[step - 1]
            )
    mask_rows((1 - chip) * 2 + core)
    chunk_rows, chunk_columns = 8, columns // 2
    for part in range(2):
        at, size, peers = axes[1 - part]
        here = pl.ds(pl.multiple_of(at * last_rows, last_rows), last_rows)
        total = first_sum[part][here, :].astype(F32)
        for step in range(1, size):
            seconds[part][step].wait_recv()
            total += second_in[part][step - 1].astype(F32)
        if z_size == 1:
            second_all[part][here, :] = total.astype(BF16)
        else:
            for block in range(4):
                r, c = block // 2 * chunk_rows, block % 2 * chunk_columns
                second_sum[part * 4 + block] = total[r : r + chunk_rows, c : c + chunk_columns]

    if z_size > 1:
        depths = {
            s: begin(second_sum.at[lax.rem(z + s, z_size)], depth_in.at[s - 1], z_peers[s - 1])
            for s in far_first(z_size)
        }
    onward.wait_recv()
    mask_rows((1 - chip) * 2 + 1 - core)
    drain()
    if z_size > 1:
        total = second_sum[z]
        for step in range(1, z_size):
            depths[step].wait_recv()
            total += depth_in[step - 1]
        depth_all[z] = total
        backs = [
            begin(depth_all.at[z], depth_all.at[z], z_peers[s - 1]) for s in far_first(z_size)
        ]
        for copy in backs:
            copy.wait_recv()
        for part in range(2):
            at = axes[1 - part][0]
            here = pl.ds(pl.multiple_of(at * last_rows, last_rows), last_rows)
            rows_of = []
            for high in range(2):
                rows_of.append(
                    jnp.concatenate(
                        [depth_all[part * 4 + high * 2], depth_all[part * 4 + high * 2 + 1]], axis=1
                    )
                )
            second_all[part][here, :] = jnp.concatenate(rows_of, axis=0).astype(BF16)

    backs = ([], [])
    for part in range(2):
        at, size, peers = axes[1 - part]
        here = pl.ds(pl.multiple_of(at * last_rows, last_rows), last_rows)
        for step in far_first(size):
            block = second_all[part].at[here, :]
            backs[part].append(begin(block, block, peers[step - 1]))
    spread = ([], [])
    for part in range(2):
        for copy in backs[part]:
            copy.wait_recv()
        at, size, peers = axes[part]
        count = counts[part]
        here = pl.ds(pl.multiple_of(at * count, count), count)
        target = gathered.at[part, core, here, :]
        for step in far_first(size):
            spread[part].append(begin(second_all[part], target, peers[step - 1]))
        gathered[part, core, here, :] = second_all[part][...]
    mirrored = []
    for part in range(2):
        for copy in spread[part]:
            copy.wait_recv()
        whole = gathered.at[part, core]
        mirrored.append(begin(whole, whole, other_core))
    drain()
    for copy in mirrored:
        copy.wait_recv()


def store_kernel(gathered_ref, rows_ref, mask_hbm, qkv_hbm, out_hbm, qkv_ref, out_ref, store):
    copies = [pltpu.make_async_copy(rows_ref, mask_hbm, store.at[0])]
    copies[0].start()
    columns = gathered_ref.shape[3]
    quarter = INNER // 4
    for block in range(3):
        here = slice(block * quarter, (block + 1) * quarter)
        there = slice(block % 2 * quarter, (block % 2 + 1) * quarter)
        for core in range(2):
            qkv_ref[here, core * columns : (core + 1) * columns] = gathered_ref[
                block // 2, core, there, :
            ].astype(F32)
        copies.append(
            pltpu.make_async_copy(qkv_ref.at[here, :], qkv_hbm.at[here, :], store.at[1 + block])
        )
        copies[-1].start()
    for block in range(4):
        out_ref[block * quarter : (block + 1) * quarter, :] = gathered_ref[
            1, block // 2, quarter:, block % 2 * D : (block % 2 + 1) * D
        ].astype(F32)
    copies.append(pltpu.make_async_copy(out_ref, out_hbm, store.at[4]))
    copies[-1].start()
    for copy in copies:
        copy.wait()


def rotary_table(tokens):
    position = (np.arange(tokens) % PAD).astype(np.float64)[None, :]
    frequency = np.exp(-math.log(10000.0) * np.arange(HALF) / HALF)[:, None]
    angles = position * frequency
    return np.concatenate([np.cos(angles), np.sin(angles)], axis=0).astype(np.float32)


def axis_sizes(tm_size):
    return {64: (4, 2, 8), 8: (4, 2, 1), 4: (4, 1, 1), 2: (2, 1, 1), 1: (1, 1, 1)}[tm_size]


def on_device(
    sizes, spectrum, band_assign, split_weight, qkv_weight, out_weight, mask_weight, mask_cotangent
):
    frames, width = spectrum.shape
    tokens = frames // 4 * PAD
    x_size, y_high, z_size = sizes
    y_size = 2 * y_high
    half, columns = INNER // 2, 2 * D
    last = half // (x_size * y_size)
    copies = 72

    def vmem(*shape, dtype=BF16):
        return pltpu.VMEM(shape, dtype)

    inside = pl.BlockSpec(memory_space=pltpu.VMEM)
    outside = pl.BlockSpec(memory_space=pltpu.HBM)
    assign = jnp.transpose(band_assign, (2, 0, 1))
    rows, gathered = pl.pallas_call(
        functools.partial(whole_kernel, sizes),
        out_shape=[
            jax.ShapeDtypeStruct((frames, width), F32),
            jax.ShapeDtypeStruct((2, 2, half, columns), BF16),
        ],
        in_specs=[outside] * 8,
        out_specs=[inside] * 2,
        scratch_shapes=[
            vmem(frames, width),
            vmem(frames, width),
            vmem(*assign.shape, dtype=jnp.int32),
            vmem(2 * HALF, tokens, dtype=F32),
            vmem(*split_weight.shape),
            vmem(*mask_weight.shape),
            vmem(*qkv_weight.shape),
            vmem(*out_weight.shape),
            vmem(width, 2 * D),
            vmem(width, 2 * D),
            vmem(frames, width, dtype=F32),
            vmem(frames, width, dtype=F32),
            vmem(PAD, width),
            vmem(PAD, width),
            vmem(1, width, dtype=F32),
            vmem(tokens, width),
            vmem(frames, 128, dtype=F32),
            vmem(3, frames, 128, dtype=F32),
            vmem(2, 4, tokens, D),
            vmem(2, 2, tokens, D),
            vmem(2, tokens, D),
            vmem(2, tokens, D),
            vmem(HEADS, tokens, tokens, dtype=F32),
            vmem(3 * INNER, tokens),
            vmem(INNER, tokens),
            vmem(3 * INNER, tokens),
            vmem(3 * INNER, D),
            vmem(D, INNER),
            vmem(tokens, tokens, dtype=F32),
            vmem(D, tokens),
            vmem(D, tokens),
            vmem(INNER // 2, tokens),
            vmem(D, tokens),
            vmem(D, tokens),
            vmem(3 * INNER // 2, tokens),
            vmem(4, tokens, D),
            vmem(tokens, 2 * D),
            vmem(2, half, columns),
            [
                vmem(max(x_size - 1, 1), half // x_size, columns),
                vmem(y_size - 1, half // y_size, columns),
            ],
            [vmem(half // x_size, columns), vmem(half // y_size, columns)],
            [vmem(y_size - 1, last, columns), vmem(max(x_size - 1, 1), last, columns)],
            vmem(8, 8, D, dtype=F32),
            vmem(7, 8, D, dtype=F32),
            vmem(8, 8, D, dtype=F32),
            [vmem(half // x_size, columns), vmem(half // y_size, columns)],
            pltpu.SemaphoreType.DMA((8,)),
            pltpu.SemaphoreType.DMA((copies,)),
            pltpu.SemaphoreType.DMA((copies,)),
        ],
        compiler_params=pltpu.CompilerParams(
            vmem_limit_bytes=VMEM_BYTES, collective_id=0, has_side_effects=True
        ),
    )(
        *(
            pltpu.with_memory_space_constraint(operand, pltpu.HBM)
            for operand in (
                spectrum,
                mask_cotangent,
                assign,
                jnp.asarray(rotary_table(tokens)),
                split_weight,
                mask_weight,
                qkv_weight,
                out_weight,
            )
        )
    )
    return tuple(
        pl.pallas_call(
            store_kernel,
            out_shape=[
                jax.ShapeDtypeStruct((frames, width), F32),
                jax.ShapeDtypeStruct(qkv_weight.shape, F32),
                jax.ShapeDtypeStruct(out_weight.shape, F32),
            ],
            in_specs=[inside] * 2,
            out_specs=[outside] * 3,
            scratch_shapes=[
                vmem(*qkv_weight.shape, dtype=F32),
                vmem(*out_weight.shape, dtype=F32),
                pltpu.SemaphoreType.DMA((5,)),
            ],
            compiler_params=pltpu.CompilerParams(vmem_limit_bytes=VMEM_BYTES // 4),
        )(gathered, rows)
    )


def solution(mesh):
    return jax.shard_map(
        functools.partial(on_device, axis_sizes(mesh.shape["tm"])),
        mesh=mesh,
        in_specs=(
            P("tm", "band"),
            P(),
            P("band", None, None, None),
            P(),
            P(),
            P("band", None, None, None),
            P("tm", "band"),
        ),
        out_specs=(P("tm", "band"), P(), P()),
        check_vma=False,
    )
```
